256 devices in a mesh: tm: 32 (over x, z_hi, core), replica: 8 (over z_lo, y).
Axes of the slice: x: 4, y: 4, z: 8 (z_hi: 4, z_lo: 2; z = z_hi * 2 + z_lo), core: 2. Of those that a mesh axis runs over, the one named last changes fastest.
Arguments:
- latents: bfloat16 [8, 32, 256, 1152], P('replica', 'tm'), may hold values from -6 to 6
- cotangent: bfloat16 [8, 32, 256, 1152], P('replica', 'tm'), may hold values from -6 to 6
- w_qkv: bfloat16 [1152, 3456], P('replica'), may hold values from -30 to 30
- w_out: bfloat16 [1152, 1152], P('replica'), may hold values from -0.1875 to 0.1875
- tile_pattern: int32 [4, 4], replicated, may hold values from 0 to 1, as said below
Outputs:
- block_output: bfloat16 [8, 32, 256, 1152], P('replica', 'tm')
- grad_latents: bfloat16 [8, 32, 256, 1152], P('replica', 'tm')
- dw_qkv: float32 [1152, 3456], P('replica')
- dw_out: float32 [1152, 1152], P('replica')
The draws below stay inside these ranges and needn't reach their ends.
Inputs may be any that keep to these rules, and one draw needn't show every extreme that they name: `tile_pattern`: every tile may attend to itself.
All inputs are finite; a program needn't handle non-finite values.
Results may differ from the reference program's by a relative error of at most 0.034.
The reference program's roundings to bfloat16 on the way count: a program that leaves them out, or rounds other values in their place, can miss the bound.
Values may be sent and summed in bfloat16 or wider, within the bound.
No kernel may reach another device: no remote copies, remote signals or barrier semaphores. Data moves between devices by JAX's collectives and lax.ppermute only.
A program may use at most 128 MiB of HBM per device.

```python
import math
import jax
import jax.numpy as jnp
from jax import lax

D = 1152
HEADS = 16
HEAD_SIZE = 72
SPATIAL_HEADS = 8
TILE = 64
TILES = 4
FRAMES = 32
SAMPLES = 8
TOKENS_FRAME = 256
TOKENS = 65536


def draw_latents(key, part):
    key = jax.random.fold_in(key, 5)
    drawn = jax.random.normal(key, (SAMPLES, FRAMES, TOKENS_FRAME, D), jnp.float32)
    return jnp.clip(drawn, -6.0, 6.0).astype(jnp.bfloat16)


def draw_w_qkv(key, part):
    key = jax.random.fold_in(key, 7)
    drawn = jnp.clip(jax.random.normal(key, (D, 3 * D), jnp.float32), -6.0, 6.0) / math.sqrt(D)
    return drawn.astype(jnp.bfloat16)


def draw_tile_pattern(key, part):
    key = jax.random.fold_in(key, 3)
    coin_flips = jax.random.randint(key, (TILES, TILES), 0, 2)
    positions = jnp.arange(TILES)
    diagonal = (positions[:, None] == positions[None, :]).astype(jnp.int32)
    return jnp.maximum(coin_flips, diagonal).astype(jnp.int32)


def block_scale(rng, dims, cuts, low, top_value):
    loudness, own = 1.0, jax.random.fold_in(rng, 6)
    for axis_at, parts in cuts:
        steps = jnp.exp(jax.random.uniform(jax.random.fold_in(own, axis_at), (parts,), jnp.float32, low / len(cuts), top_value / len(cuts)))
        loudness = loudness * jnp.repeat(steps, dims[axis_at] // parts).reshape([-1 if axis == axis_at else 1 for axis in range(len(dims))])
    return loudness


def scatter_about(own_key, shape, scale, reach, split=(), held_as=jnp.bfloat16):
    level = block_scale(own_key, shape, split, -0.22, 0.18) if split else 1.0
    array = jax.random.normal(own_key, shape, jnp.float32) * scale * level
    return jnp.minimum(jnp.maximum(array, -reach), reach).astype(held_as)


def setup_inputs(seed: int = 0) -> dict:
    seeds = jax.random.split(jax.random.key(seed), 6)
    latents = draw_latents(jax.random.fold_in(seeds[5], 71), 0)
    cotangent = scatter_about(seeds[1], (SAMPLES, FRAMES, TOKENS_FRAME, D), 1.0, 6.0, ((0, 8), (1, 32)))
    w_qkv = draw_w_qkv(jax.random.fold_in(seeds[5], 71), 0)
    w_out = scatter_about(seeds[3], (D, D), D ** -0.5, 0.1875, ((0, 8),))
    tile_pattern = draw_tile_pattern(jax.random.fold_in(seeds[5], 71), 0)
    return dict(latents=latents, cotangent=cotangent, w_qkv=w_qkv, w_out=w_out, tile_pattern=tile_pattern)


def normalize(inputs):
    average = lax.optimization_barrier(jnp.mean(inputs, -1, keepdims=True))
    centred = inputs - average
    spread = lax.optimization_barrier(jnp.mean(centred * centred, -1, keepdims=True))
    inverse_std = lax.rsqrt(spread + 1e-06)
    return (centred * inverse_std, inverse_std)

def attend_forward(queries, keys_in, values_in, allowed, layout):
    key_layout = layout.replace('q', 'k')
    factor = 1.0 / math.sqrt(queries.shape[-1])
    scores = jnp.einsum(layout + ',' + key_layout + '->ghqk', queries.astype(jnp.float32), keys_in.astype(jnp.float32)) * factor
    scores = jnp.where(allowed, scores, -1e+30)
    row_max = lax.optimization_barrier(jnp.max(scores, -1, keepdims=True))
    weights = jnp.exp(scores - row_max)
    probs = weights / lax.optimization_barrier(jnp.sum(weights, -1, keepdims=True))
    rounded = probs.astype(jnp.bfloat16)
    mixed = jnp.einsum('ghqk,' + key_layout + '->' + layout, rounded.astype(jnp.float32), values_in.astype(jnp.float32))
    return (mixed.astype(jnp.bfloat16), probs, rounded)

def attend_backward(queries, keys_in, values_in, probs, rounded, upstream, layout):
    key_layout = layout.replace('q', 'k')
    factor = 1.0 / math.sqrt(queries.shape[-1])
    grad_probs = jnp.einsum(layout + ',' + key_layout + '->ghqk', upstream.astype(jnp.float32), values_in.astype(jnp.float32))
    grad_values = jnp.einsum('ghqk,' + layout + '->' + key_layout, rounded.astype(jnp.float32), upstream.astype(jnp.float32)).astype(jnp.bfloat16)
    centre = lax.optimization_barrier(jnp.sum(probs * grad_probs, -1, keepdims=True))
    grad_scores = (probs * (grad_probs - centre) * factor).astype(jnp.bfloat16)
    grad_queries = jnp.einsum('ghqk,' + key_layout + '->' + layout, grad_scores.astype(jnp.float32), keys_in.astype(jnp.float32)).astype(jnp.bfloat16)
    grad_keys = jnp.einsum('ghqk,' + layout + '->' + key_layout, grad_scores.astype(jnp.float32), queries.astype(jnp.float32)).astype(jnp.bfloat16)
    return (grad_queries, grad_keys, grad_values)

def sample_pass(sample, upstream, w_qkv, w_out, allowed):
    frames, tokens, width = sample.shape
    spatial_cols = SPATIAL_HEADS * HEAD_SIZE
    temporal_cols = width - spatial_cols
    temporal_heads = HEADS - SPATIAL_HEADS
    inputs = sample.astype(jnp.float32)
    normed, inverse_std = normalize(inputs)
    hidden = normed.astype(jnp.bfloat16)
    projected = jnp.dot(hidden.reshape(-1, width), w_qkv, preferred_element_type=jnp.float32).astype(jnp.bfloat16)
    projected = projected.reshape(frames, tokens, 3 * width)

    def spatial_part(offset):
        return projected[:, :, offset:offset + spatial_cols].reshape(frames, tokens, SPATIAL_HEADS, HEAD_SIZE)

    def temporal_part(offset):
        return projected[:, :, offset + spatial_cols:offset + width].reshape(frames, tokens, temporal_heads, HEAD_SIZE)
    space_query, space_key, space_value = (spatial_part(0), spatial_part(width), spatial_part(2 * width))
    time_query, time_key, time_value = (temporal_part(0), temporal_part(width), temporal_part(2 * width))
    time_mask = jnp.ones((frames, frames), jnp.bool_)
    space_out, space_probs, space_round = attend_forward(space_query, space_key, space_value, allowed, 'gqhe')
    time_out, time_probs, time_round = attend_forward(time_query, time_key, time_value, time_mask, 'qghe')
    attended = jnp.concatenate([space_out.reshape(frames, tokens, spatial_cols), time_out.reshape(frames, tokens, temporal_cols)], -1)
    mixed = jnp.dot(attended.reshape(-1, width), w_out, preferred_element_type=jnp.float32).reshape(frames, tokens, width)
    result = (inputs + mixed).astype(jnp.bfloat16)
    grad_attended = jnp.dot(upstream.reshape(-1, width), w_out.T, preferred_element_type=jnp.float32).astype(jnp.bfloat16)
    grad_attended = grad_attended.reshape(frames, tokens, width)
    space_up = grad_attended[:, :, :spatial_cols].reshape(frames, tokens, SPATIAL_HEADS, HEAD_SIZE)
    time_up = grad_attended[:, :, spatial_cols:].reshape(frames, tokens, temporal_heads, HEAD_SIZE)
    space_gq, space_gk, space_gv = attend_backward(space_query, space_key, space_value, space_probs, space_round, space_up, 'gqhe')
    time_gq, time_gk, time_gv = attend_backward(time_query, time_key, time_value, time_probs, time_round, time_up, 'qghe')

    def flat_space(block):
        return block.reshape(frames, tokens, spatial_cols)

    def flat_time(block):
        return block.reshape(frames, tokens, temporal_cols)
    grad_proj = jnp.concatenate([flat_space(space_gq), flat_time(time_gq), flat_space(space_gk), flat_time(time_gk), flat_space(space_gv), flat_time(time_gv)], -1)
    grad_hidden = jnp.dot(grad_proj.reshape(-1, 3 * width), w_qkv.T, preferred_element_type=jnp.float32).reshape(frames, tokens, width)
    grad_mean = lax.optimization_barrier(jnp.mean(grad_hidden, -1, keepdims=True))
    grad_dot = lax.optimization_barrier(jnp.mean(grad_hidden * normed, -1, keepdims=True))
    grad_input = (upstream.astype(jnp.float32) + inverse_std * (grad_hidden - grad_mean - normed * grad_dot)).astype(jnp.bfloat16)

    def accumulate(carry, frame_parts):
        frame_hidden, frame_grad, frame_mixed, frame_upstream = frame_parts
        term_qkv = jnp.dot(frame_grad.T, frame_hidden, preferred_element_type=jnp.float32)
        term_out = jnp.dot(frame_upstream.T, frame_mixed, preferred_element_type=jnp.float32)
        rounded_qkv = lax.optimization_barrier(term_qkv.astype(jnp.bfloat16))
        rounded_out = lax.optimization_barrier(term_out.astype(jnp.bfloat16))
        return ((carry[0] + rounded_qkv.astype(jnp.float32), carry[1] + rounded_out.astype(jnp.float32)), None)
    start_sums = (jnp.zeros((3 * width, width), jnp.float32), jnp.zeros((width, width), jnp.float32))
    totals, unused = lax.scan(accumulate, start_sums, (hidden, grad_proj, attended, upstream))
    return (result, grad_input, totals[0], totals[1])

def reference(latents, cotangent, w_qkv, w_out, tile_pattern):
    allowed = jnp.repeat(jnp.repeat(tile_pattern, TILE, 0), TILE, 1) > 0

    def one_sample(pair):
        return sample_pass(pair[0], pair[1], w_qkv, w_out, allowed)
    outputs, grads, qkv_terms, out_terms = lax.map(one_sample, (latents, cotangent))
    factor = 1.0 / math.sqrt(TOKENS)
    dw_qkv = (lax.optimization_barrier(jnp.sum(qkv_terms, 0)) * factor).T
    dw_out = (lax.optimization_barrier(jnp.sum(out_terms, 0)) * factor).T
    return (outputs, grads, dw_qkv, dw_out)
```

```python
import math

import jax
import jax.numpy as jnp
from jax import lax
from jax.experimental import pallas as pl
from jax.experimental.pallas import tpu as pltpu
from jax.sharding import PartitionSpec as P

HEADS = 16
HEAD_SIZE = 72
SPATIAL_HEADS = 8
TOK = 256
D = 1152
HALF = 640
TOFF = 512
ROWS = 144
BF = jnp.bfloat16
F32 = jnp.float32
NEG = -1e30
VMEM_LIMIT = 60 * 1024 * 1024
AXES = ("tm", "replica")
HBM = pl.BlockSpec(memory_space=pl.ANY)
VM = pl.BlockSpec(memory_space=pltpu.VMEM)
SM = pl.BlockSpec(memory_space=pltpu.SMEM)
PARAMS = pltpu.CompilerParams(vmem_limit_bytes=VMEM_LIMIT)


def nn(a, b):
    return lax.dot_general(a, b, (((1,), (0,)), ((), ())), preferred_element_type=F32)


def nt(a, b):
    return lax.dot_general(a, b, (((1,), (1,)), ((), ())), preferred_element_type=F32)


def tn(a, b):
    return lax.dot_general(a, b, (((0,), (0,)), ((), ())), preferred_element_type=F32)


def normalize(x):
    x = x.astype(F32)
    centred = x - jnp.mean(x, -1, keepdims=True)
    r = lax.rsqrt(jnp.mean(centred * centred, -1, keepdims=True) + 1e-06)
    return centred * r, r


def norm_kernel(src_ref, h_ref, ht_ref):
    n, _ = normalize(src_ref[...])
    h_ref[...] = n.astype(BF)
    ht_ref[...] = n.T.astype(BF)


def norm_call(src):
    s = jax.ShapeDtypeStruct
    outs = (s((TOK, D), BF), s((D, TOK), BF))
    return pl.pallas_call(
        norm_kernel,
        out_shape=outs,
        in_specs=[VM],
        out_specs=(VM,) * len(outs),
        compiler_params=PARAMS,
        cost_estimate=pl.CostEstimate(flops=10**8, bytes_accessed=2 * 10**6, transcendentals=0),
        name="norm",
    )(src)


def attend_kernel(kind, plan, n_piece, *refs):
    coord, mask_ref, hid_ref, cot_ref = refs[:4]
    pieces = refs[4 : 4 + n_piece]
    outs = refs[4 + n_piece : -5]
    if kind == 1:
        normed, _ = normalize(hid_ref[:, :D])
        hid = normed.astype(BF)
        cot = hid_ref[:, D:]
        outs[3][...] = normed.T.astype(BF)
        outs[4][...] = cot
    else:
        hid, cot = hid_ref[...], cot_ref[...]
    w, wo, g4, sem, wo_sem = refs[-5:]
    keep_ref, send_ref = outs[:2]
    core, zl, y = coord[0], coord[1], coord[2]
    lo = kind * TOFF
    cols = slice(lo, lo + HALF)
    copies = []
    for n, (view, quarter, dz, dy) in enumerate(plan):
        own, add, count = quarter
        rep = lax.rem(zl + dz, 2) * 4 + lax.rem(y + dy, 4)
        rows = pl.ds(pl.multiple_of(rep * ROWS, 16), ROWS)
        src = view(pieces)
        for k in range(count):
            part = src.at[k] if count > 1 else src
            if own == "abs":
                if add == 3:
                    c = pltpu.make_async_copy(part, wo.at[rows, :], sem.at[n, k])
                else:
                    c = pltpu.make_async_copy(part.at[:, cols], w.at[add, rows, :], sem.at[n, k])
                c.start()
                copies.append(c)
                continue
            j = k + add
            second = core if own == "own" else 1 - core
            if j == 0:
                c = pltpu.make_async_copy(part.at[:, cols], w.at[2 * second, rows, :], sem.at[n, k])
                c.start()
                copies.append(c)
            else:
                to_w = pltpu.make_async_copy(part.at[:, cols], w.at[1, rows, :], sem.at[n, k])
                to_o = pltpu.make_async_copy(part, wo.at[rows, :], sem.at[n, k])
                pl.when(second == 0)(to_w.start)
                pl.when(second == 1)(to_o.start)
                copies.append((second, to_w, to_o))
    for c in copies:
        if isinstance(c, tuple):
            pl.when(c[0] == 0)(c[1].wait)
            pl.when(c[0] == 1)(c[2].wait)
        else:
            c.wait()
    if kind == 0:
        out_copy = pltpu.make_async_copy(wo, outs[4], wo_sem)
        out_copy.start()
    factor = 1.0 / math.sqrt(HEAD_SIZE)
    q = nn(hid, w[0]).astype(BF)
    k = nn(hid, w[1]).astype(BF)
    v = nn(hid, w[2]).astype(BF)
    u = nt(cot, wo[cols, :]).astype(BF)
    allowed = mask_ref[...] > 0
    sums = [[None] * 5 for _ in range(4)]
    for h in range(8):
        s = kind * 64 + HEAD_SIZE * h
        t0, t1 = s // 128, (s + HEAD_SIZE - 1) // 128 + 1
        win = slice(t0 * 128, t1 * 128)
        lane = lax.broadcasted_iota(jnp.int32, (1, (t1 - t0) * 128), 1) + t0 * 128
        ours = jnp.logical_and(lane >= s, lane < s + HEAD_SIZE).astype(F32).astype(BF)
        qh, kh, vh, uh = (a[:, win] * ours for a in (q, k, v, u))
        sc = jnp.where(allowed, nt(qh, kh) * factor, NEG)
        e = jnp.exp(sc - jnp.max(sc, -1, keepdims=True))
        p = e * (1.0 / jnp.sum(e, -1, keepdims=True))
        pb = p.astype(BF)
        gp = nt(uh, vh)
        pg = p * gp
        gs = ((pg - p * jnp.sum(pg, -1, keepdims=True)) * factor).astype(BF)
        res = (nn(gs, kh), tn(gs, qh), tn(pb, uh), nn(pb, vh))
        for j, r in enumerate(res):
            for t in range(t0, t1):
                part = r[:, (t - t0) * 128 : (t - t0 + 1) * 128]
                sums[j][t] = part if sums[j][t] is None else sums[j][t] + part
        for t in range(5):
            if s < (t + 1) * 128 <= s + HEAD_SIZE or (h == 7 and t == 4):
                for j in range(4):
                    g4[j // 2, j % 2, :, t * 128 : (t + 1) * 128] = sums[j][t].astype(BF)
    gh = nt(g4[0, 0], w[0]) + nt(g4[0, 1], w[1]) + nt(g4[1, 0], w[2])
    if kind == 0:
        outs[2][...] = g4[1, 1]
        outs[3][...] = gh
    else:
        outs[2][:, :HALF] = g4[1, 1]
        outs[2][:, HALF:] = gh.astype(BF)
    keep_ref[...] = g4[core]
    send_ref[...] = g4[1 - core]
    if kind == 0:
        out_copy.wait()


def attend_call(kind, coord, mask, hid, cot, pieces, plan):
    s = jax.ShapeDtypeStruct
    both = s((2, TOK, HALF), BF)
    if kind == 0:
        outs, specs = (s((TOK, HALF), BF), s((TOK, D), F32), s((D, D), BF)), (VM, VM, HBM)
    else:
        outs, specs = (s((TOK, HALF + D), BF), s((D, TOK), BF), s((TOK, D), BF)), (VM,) * 3
    return pl.pallas_call(
        lambda *refs: attend_kernel(kind, plan, len(pieces), *refs),
        out_shape=(both, both) + outs,
        in_specs=[SM] + [VM] * 3 + [HBM] * len(pieces),
        out_specs=(VM, VM) + specs,
        scratch_shapes=[
            pltpu.VMEM((3, D, HALF), BF),
            pltpu.VMEM((D, D), BF),
            pltpu.VMEM((2, 2, TOK, HALF), BF),
            pltpu.SemaphoreType.DMA((len(plan), 2)),
            pltpu.SemaphoreType.DMA,
        ],
        compiler_params=PARAMS,
        cost_estimate=pl.CostEstimate(flops=6 * 10**9, bytes_accessed=16 * 10**6, transcendentals=10**6),
        name=("attend_space", "attend_time")[kind],
    )(coord, mask, hid, cot, *pieces)


SHIP0 = ((0, (1, 2)), (0, (0, 3)), (1, (3, 2)), (1, (0, 1)))
SHIP1 = ((1, (0, 1)), (1, (2, 3)), (0, (0, 1, 2, 3)))


def weight_kernel(coord, hft, hpt, hft2, hpt2, cf, cp, cf2, cp2, kf, kp, rf, rp, *refs):
    outs, (a0, a1, sem) = refs[:7], refs[7:]
    core, zl, y = coord[0], coord[1], coord[2]

    def by_hidden(x, out):
        tiles = [((0, 256), None), ((256, 512), None), ((512, 640), (0, 128)), (None, (128, 384)), (None, (384, 640))]
        at = 0
        for f, p in tiles:
            parts = []
            if f is not None:
                sl = slice(*f)
                parts += [nn(hft[...], kf[x, :, sl]), nn(hft2[...], rf[x, :, sl])]
            if p is not None:
                sl = slice(*p)
                parts += [nn(hpt[...], kp[x, :, sl]), nn(hpt2[...], rp[x, :, sl])]
            total = sum(parts[1:], parts[0])
            out[:, at : at + total.shape[1]] = total.astype(BF)
            at += total.shape[1]

    def by_attended(x, out):
        for c in range(0, D, 384):
            sl = slice(c, c + 384)
            f = tn(kf[x], cf[:, sl]) + tn(rf[x], cf2[:, sl])
            p = tn(kp[x], cp[:, sl]) + tn(rp[x], cp2[:, sl])
            out[0:512, sl] = f[:512].astype(BF)
            out[512:640, sl] = (f[512:] + p[:128]).astype(BF)
            out[640:1152, sl] = p[128:].astype(BF)

    def ship(scratch, ships, refs, n):
        copies = []
        for r, ((a, order), out) in enumerate(zip(ships, refs)):
            for i, j in enumerate(order):
                rep = lax.rem(zl + a, 2) * 4 + jnp.bitwise_xor(y, j)
                rows = pl.ds(pl.multiple_of(rep * ROWS, 16), ROWS)
                c = pltpu.make_async_copy(scratch.at[rows, :], out.at[i], sem.at[n, r, i])
                c.start()
                copies.append(c)
        return copies

    by_hidden(0, a0)
    c0 = ship(a0, SHIP0, outs[:4], 0)

    @pl.when(core == 0)
    def _():
        by_hidden(1, a1)

    @pl.when(core == 1)
    def _():
        by_attended(1, a1)

    c1 = ship(a1, SHIP1, outs[4:], 1)
    for c in c0 + c1:
        c.wait()


def weight_call(coord, *args):
    outs = tuple(jax.ShapeDtypeStruct((len(o), ROWS, D), BF) for _, o in SHIP0 + SHIP1)
    return pl.pallas_call(
        weight_kernel,
        out_shape=outs,
        in_specs=[SM] + [VM] * len(args),
        out_specs=(HBM,) * len(outs),
        scratch_shapes=[pltpu.VMEM((D, D), BF), pltpu.VMEM((D, D), BF), pltpu.SemaphoreType.DMA((2, 4, 4))],
        compiler_params=PARAMS,
        cost_estimate=pl.CostEstimate(flops=6 * 10**9, bytes_accessed=16 * 10**6, transcendentals=0),
        name="weight_grads",
    )(coord, *args)


def finish_kernel(lat_ref, cot_ref, att_ref, ghf_ref, back_ref, wo_ref, out_ref, gl_ref):
    lat = lat_ref[...]
    mixed = nn(att_ref[...], wo_ref[0:HALF, :]) + nn(back_ref[:, :HALF], wo_ref[TOFF:D, :])
    out_ref[...] = (lat.astype(F32) + mixed).astype(BF)
    normed, r = normalize(lat)
    gh = ghf_ref[...] + back_ref[:, HALF:].astype(F32)
    mean = jnp.mean(gh, -1, keepdims=True)
    dot = jnp.mean(gh * normed, -1, keepdims=True)
    gl_ref[...] = (cot_ref[...].astype(F32) + r * (gh - mean - normed * dot)).astype(BF)


def finish_call(*args):
    s = jax.ShapeDtypeStruct((TOK, D), BF)
    return pl.pallas_call(
        finish_kernel,
        out_shape=(s, s),
        in_specs=[VM] * 6,
        out_specs=(VM, VM),
        compiler_params=PARAMS,
        cost_estimate=pl.CostEstimate(flops=10**9, bytes_accessed=8 * 10**6, transcendentals=0),
        name="finish",
    )(*args)


def pairs(move):
    out = []
    for x in range(4):
        for z in range(8):
            for c in range(2):
                for y in range(4):
                    to = move(x, y, z, c)
                    spot = []
                    for xx, yy, zz, cc in ((x, y, z, c), (to[0] % 4, to[1] % 4, to[2] % 8, to[3])):
                        spot.append(((xx * 4 + zz // 2) * 2 + cc) * 8 + (zz % 2) * 4 + yy)
                    out.append(tuple(spot))
    return out


CORE = pairs(lambda x, y, z, c: (x, y, z, 1 - c))
XP = [pairs(lambda x, y, z, c, d=d: (x + d, y, z, c)) for d in range(4)]
YP = [pairs(lambda x, y, z, c, d=d: (x, y + d, z, c)) for d in range(4)]
ZP = [pairs(lambda x, y, z, c, d=d: (x, y, z + d, c)) for d in range(8)]
Y1 = pairs(lambda x, y, z, c: (x, y ^ 1, z, c))
Y3 = pairs(lambda x, y, z, c: (x, y ^ 3, z, c))
Z1 = pairs(lambda x, y, z, c: (x, y, z ^ 1, c))
Z1B = pairs(lambda x, y, z, c: (x, y, (z + 1 if z % 2 else z - 1), c))


def move(a, p):
    return lax.ppermute(a, AXES, p)


def add(*terms):
    total = terms[0].astype(F32)
    for t in terms[1:]:
        total = total + t.astype(F32)
    return total


def gather_weights(w_qkv, w_out, core, early):
    first = core == 0
    cols = [w_qkv[:, :D], w_qkv[:, D : 2 * D], w_qkv[:, 2 * D :], w_out]
    own = jnp.stack([jnp.where(first, cols[0], cols[2]), jnp.where(first, cols[1], cols[3])])
    pieces, plan = [w_qkv, w_out], []
    for q in range(3):
        plan.append((lambda r, q=q: r[0].at[:, q * D : (q + 1) * D], ("abs", q, 1), 0, 0))
    plan.append((lambda r: r[1], ("abs", 3, 1), 0, 0))

    def note(array, side, add, dz, dy):
        i = len(pieces)
        pieces.append(array)
        count = 2 if array.ndim == 3 else 1
        plan.append((lambda r, i=i: r[i], (side, add, count), dz, dy))

    def both(array, add, dz, dy):
        note(array, "own", add, dz, dy)
        note(move(array, CORE), "other", add, dz, dy)

    za, zb = move(own[0], ZP[1]), move(own[1], ZP[7])
    up, down = move(own, YP[1]), move(own, YP[3])
    lat_cot, *early = early
    za, zb, lat_cot = lax.optimization_barrier((za, zb, lat_cot))
    pos = lax.all_to_all(lat_cot, "tm", split_axis=0, concat_axis=0, tiled=True).reshape(TOK, 2 * D)
    z = jnp.stack([za, zb])
    zup, zdown = move(z, YP[1]), move(z, YP[3])
    up, down, *early = lax.optimization_barrier((up, down, *early))
    both(z, 0, 1, 0)
    both(up, 0, 0, 3)
    both(down, 0, 0, 1)
    both(zup, 0, 1, 3)
    both(zdown, 0, 1, 1)
    both(move(up[0], YP[1]), 0, 0, 2)
    both(move(down[1], YP[3]), 1, 0, 2)
    both(move(zup[0], YP[1]), 0, 1, 2)
    both(move(zdown[1], YP[3]), 1, 1, 2)
    return pieces, plan, pos, early


def all_sum(own):
    x = lax.axis_index("tm") // 8
    parts = own.reshape(4, 72, D)

    def part(i):
        return lax.dynamic_index_in_dim(parts, i % 4, 0, keepdims=False)

    got = [move(part(x + d), XP[d]) for d in (1, 2, 3)]
    mine = add(part(x), *got).astype(BF)
    two, four, six = (move(mine, ZP[d]) for d in (2, 4, 6))
    row = (add(mine, four) + add(two, six)).astype(BF)
    ring = jnp.stack([row] + [move(row, XP[d]) for d in (1, 2, 3)])
    return jnp.take(ring, (x - jnp.arange(4)) % 4, axis=0).reshape(2, ROWS, D)


def reduce_out0(s0a, k0a, s0b, k0b):
    ga, gb = move(s0a, Y1), move(s0b, Y3)
    ka, kb = add(k0a, ga).astype(BF), add(k0b, gb).astype(BF)
    ga, gb = move(ka[1], Y3), move(kb[1], Y1)
    ours, theirs = add(ka[0], ga), add(kb[0], gb).astype(BF)
    return add(ours, move(theirs, Z1)).astype(BF)


def reduce_out1(sa, sb, keep):
    ga, gb = move(sa, Z1), move(sb, Z1B)
    b = [add(keep[0], ga[0]), add(keep[1], ga[1]), add(keep[2], gb[0]), add(keep[3], gb[1])]
    b = [t.astype(BF) for t in b]
    top, low = [t[:72] for t in b], [t[72:] for t in b]
    gt = move(jnp.stack([top[1], top[2]]), Y1)
    gl = move(jnp.stack([low[3], low[2]]), Y3)
    t0, t3 = add(top[0], gt[0]).astype(BF), add(top[3], gt[1]).astype(BF)
    l0, l1 = add(low[0], gl[0]).astype(BF), add(low[1], gl[1]).astype(BF)
    gt, gl = move(t3, Y3), move(l1, Y1)
    return jnp.concatenate([add(t0, gt), add(l0, gl)]).astype(BF)


def local(latents, cotangent, w_qkv, w_out, tile_pattern):
    tm, rep = lax.axis_index("tm"), lax.axis_index("replica")
    core, zl, y = tm % 2, rep // 4, rep % 4
    coord = jnp.stack([core, zl, y]).astype(jnp.int32)
    lat, cot = latents.reshape(TOK, D), cotangent.reshape(TOK, D)
    space = jnp.repeat(jnp.repeat(tile_pattern, 64, 0), 64, 1).astype(F32)
    spot = jnp.arange(TOK) % 8
    time = (spot[:, None] == spot[None, :]).astype(F32)

    lat_cot = jnp.concatenate([lat, cot], 1).reshape(32, 8, 2 * D)
    early = (lat_cot, coord, space, time, *norm_call(lat), move(cot, CORE))
    pieces, plan, pos, early = gather_weights(w_qkv, w_out, core, early)
    coord, space, time, hf, hft, cf2 = early
    hft2 = move(hft, CORE)

    kp, sp, back, hpt, cp = attend_call(1, coord, time, pos, pos, pieces, plan)
    rp, hpt2, cp2 = move(sp, CORE), move(hpt, CORE), move(cp, CORE)
    back = lax.all_to_all(
        back.reshape(32, 8, HALF + D), "tm", split_axis=0, concat_axis=0, tiled=True
    ).reshape(TOK, HALF + D)
    hf, sp = lax.optimization_barrier((hf, sp))
    kf, sf, att, ghf, wo = attend_call(0, coord, space, hf, cot, pieces, plan)
    sf, rp, hpt2, cp2, hft2 = lax.optimization_barrier((sf, rp, hpt2, cp2, hft2))
    rf = move(sf, CORE)
    w = weight_call(coord, hft, hpt, hft2, hpt2, cot, cp, cf2, cp2, kf, kp, rf, rp)
    *w, back = lax.optimization_barrier((*w, back))
    own = jnp.concatenate([reduce_out0(*w[:4]), reduce_out1(*w[4:])])
    result, grad_input = finish_call(lat, cot, att, ghf, back, wo)
    total = all_sum(own)
    other = move(total, CORE)
    factor = 1.0 / math.sqrt(65536)
    first = core == 0
    q, k = (jnp.where(first, total[i], other[i]) for i in range(2))
    v, o = (jnp.where(first, other[i], total[i]) for i in range(2))
    dw_qkv = jnp.concatenate([q, k, v], 1).astype(F32) * factor
    dw_out = o.astype(F32) * factor
    return result.reshape(1, 1, TOK, D), grad_input.reshape(1, 1, TOK, D), dw_qkv, dw_out


def solution(mesh):
    tokens, rows = P("replica", "tm", None, None), P("replica", None)
    return jax.shard_map(
        local,
        mesh=mesh,
        in_specs=(tokens, tokens, rows, rows, P()),
        out_specs=(tokens, tokens, rows, rows),
        check_vma=False,
    )
```

```python
import math

import jax
import jax.numpy as jnp
from jax import lax
from jax.experimental import pallas as pl
from jax.experimental.pallas import tpu as pltpu
from jax.sharding import PartitionSpec as P

HEADS = 16
HEAD_SIZE = 72
SPATIAL_HEADS = 8
TOK = 256
D = 1152
HALF = 640
TOFF = 512
ROWS = 144
BF = jnp.bfloat16
F32 = jnp.float32
NEG = -1e30
VMEM_LIMIT = 60 * 1024 * 1024
AXES = ("tm", "replica")
HBM = pl.BlockSpec(memory_space=pl.ANY)
VM = pl.BlockSpec(memory_space=pltpu.VMEM)
SM = pl.BlockSpec(memory_space=pltpu.SMEM)
PARAMS = pltpu.CompilerParams(vmem_limit_bytes=VMEM_LIMIT)


def nn(a, b):
    return lax.dot_general(a, b, (((1,), (0,)), ((), ())), preferred_element_type=F32)


def nt(a, b):
    return lax.dot_general(a, b, (((1,), (1,)), ((), ())), preferred_element_type=F32)


def tn(a, b):
    return lax.dot_general(a, b, (((0,), (0,)), ((), ())), preferred_element_type=F32)


def normalize(x):
    x = x.astype(F32)
    centred = x - jnp.mean(x, -1, keepdims=True)
    r = lax.rsqrt(jnp.mean(centred * centred, -1, keepdims=True) + 1e-06)
    return centred * r, r


def pack_kernel(coord, wqkv_ref, wout_ref, e_ref, g_ref):
    q, k, v = 0, D, 2 * D

    @pl.when(coord[0] == 0)
    def _():
        e_ref[0, :, 0:640] = wqkv_ref[:, q : q + 640]
        e_ref[0, :, 640:768] = wqkv_ref[:, k : k + 128]
        e_ref[1, :, 0:512] = wqkv_ref[:, k + 128 : k + 640]
        e_ref[1, :, 512:768] = wqkv_ref[:, v : v + 256]
        g_ref[:, 0:512] = wqkv_ref[:, q + 640 : q + D]
        g_ref[:, 512:768] = wqkv_ref[:, v + 640 : v + 896]

    @pl.when(coord[0] == 1)
    def _():
        e_ref[0, :, 0:384] = wqkv_ref[:, v + 256 : v + 640]
        e_ref[0, :, 384:768] = wout_ref[:, 0:384]
        e_ref[1, :, :] = wout_ref[:, 384:]
        g_ref[:, 0:512] = wqkv_ref[:, k + 640 : k + D]
        g_ref[:, 512:768] = wqkv_ref[:, v + 896 : v + D]


def pack_call(coord, w_qkv, w_out):
    s = jax.ShapeDtypeStruct
    return pl.pallas_call(
        pack_kernel,
        out_shape=(s((2, ROWS, 768), BF), s((ROWS, 768), BF)),
        in_specs=[SM, VM, VM],
        out_specs=(VM, VM),
        compiler_params=PARAMS,
        cost_estimate=pl.CostEstimate(flops=0, bytes_accessed=2 * 10**6, transcendentals=0),
        name="pack",
    )(coord, w_qkv, w_out)


def norm_kernel(tile_ref, src_ref, h_ref, ht_ref, mask_ref):
    n, _ = normalize(src_ref[...])
    h_ref[...] = n.astype(BF)
    ht_ref[...] = n.T.astype(BF)
    row = lax.broadcasted_iota(jnp.int32, (TOK, TOK), 0)
    col = lax.broadcasted_iota(jnp.int32, (TOK, TOK), 1)
    mask_ref[1] = (row % 8 == col % 8).astype(F32)
    col = lax.broadcasted_iota(jnp.int32, (64, TOK), 1) // 64
    for i in range(4):
        line = jnp.zeros((64, TOK), F32)
        for j in range(4):
            line = jnp.where(col == j, (tile_ref[i, j] == 1).astype(F32), line)
        mask_ref[0, 64 * i : 64 * (i + 1), :] = line


def norm_call(tile_pattern, src):
    s = jax.ShapeDtypeStruct
    outs = (s((TOK, D), BF), s((D, TOK), BF), s((2, TOK, TOK), F32))
    return pl.pallas_call(
        norm_kernel,
        out_shape=outs,
        in_specs=[SM, VM],
        out_specs=(VM,) * len(outs),
        compiler_params=PARAMS,
        cost_estimate=pl.CostEstimate(flops=10**8, bytes_accessed=2 * 10**6, transcendentals=0),
        name="norm",
    )(tile_pattern, src)


SPREAD = {
    "e0": (((0, 640, 0, 0), (640, 768, 1, 0)), ((0, 384, 2, 256), (384, 768, 3, 0))),
    "e1": (((0, 512, 1, 128), (512, 768, 2, 0)), ((0, 768, 3, 384),)),
    "g": (((0, 512, 0, 128), (512, 768, 2, 128)), ((0, 512, 1, 128), (512, 768, 2, 384))),
}


def load_weights(plan, pieces, w, wo, sem, coord):
    core, zl, y = coord[0], coord[1], coord[2]
    waits = []
    for n, (view, name, other, dz, dy) in enumerate(plan):
        rep = lax.rem(zl + dz, 2) * 4 + lax.rem(y + dy, 4)
        rows = pl.ds(pl.multiple_of(rep * ROWS, 16), ROWS)
        src = view(pieces)
        owner = 1 - core if other else core
        for c, spread in enumerate(SPREAD[name]):
            copies = []
            for k, (c0, c1, quarter, to) in enumerate(spread):
                dst = wo.at[rows, to : to + c1 - c0] if quarter == 3 else w.at[quarter, rows, to : to + c1 - c0]
                copies.append(pltpu.make_async_copy(src.at[:, c0:c1], dst, sem.at[n, k]))

            @pl.when(owner == c)
            def _(copies=copies):
                for d in copies:
                    d.start()

            waits.append((owner == c, copies))

    def wait():
        for when, copies in waits:

            @pl.when(when)
            def _(copies=copies):
                for d in copies:
                    d.wait()

    return wait


def attend_kernel(kind, plan, n_piece, *refs):
    coord, mask_ref, hid_ref, cot_ref, wqkv_ref, wout_ref, edge_ref = refs[:7]
    pieces = refs[7 : 7 + n_piece]
    outs = refs[7 + n_piece : -5]
    w, wo, g4, sem, own_sem = refs[-5:]
    keep_ref, send_ref = outs[:2]
    core, zl, y = coord[0], coord[1], coord[2]
    cols = slice(kind * TOFF, kind * TOFF + HALF)
    wait = load_weights(plan, pieces, w, wo, sem, coord)
    rows = pl.ds(pl.multiple_of((zl * 4 + y) * ROWS, 16), ROWS)
    copies = []
    for t in range(3):
        if kind == 0:
            src, dst = wqkv_ref.at[:, t * D : t * D + HALF], w.at[t, rows, :]
        else:
            src, dst = wqkv_ref.at[:, t * D + HALF : (t + 1) * D], w.at[t, rows, 128:]
            copies.append(pltpu.make_async_copy(edge_ref.at[t], w.at[t, :, 0:128], own_sem.at[4 + t]))
        copies.append(pltpu.make_async_copy(src, dst, own_sem.at[t]))
    if kind == 0:
        copies.append(pltpu.make_async_copy(wout_ref, wo.at[rows, :], own_sem.at[3]))
    else:
        copies.append(pltpu.make_async_copy(wout_ref, wo, own_sem.at[3]))
    for c in copies:
        c.start()
    if kind == 1:
        normed, _ = normalize(hid_ref[:, :D])
        hid = normed.astype(BF)
        cot = hid_ref[:, D:]
        outs[3][...] = normed.T.astype(BF)
        outs[4][...] = cot
    else:
        hid, cot = hid_ref[...], cot_ref[...]
    for c in copies:
        c.wait()
    wait()
    if kind == 0:
        backs = [pltpu.make_async_copy(wo, outs[4], own_sem.at[3])]
        for t in range(3):
            backs.append(pltpu.make_async_copy(w.at[t, :, TOFF:HALF], outs[5].at[t], own_sem.at[t]))
        for c in backs:
            c.start()
    factor = 1.0 / math.sqrt(HEAD_SIZE)
    q = nn(hid, w[0]).astype(BF)
    k = nn(hid, w[1]).astype(BF)
    v = nn(hid, w[2]).astype(BF)
    u = nt(cot, wo[cols, :]).astype(BF)
    allowed = mask_ref[kind] > 0
    sums = [[None] * 5 for _ in range(4)]
    for h in range(8):
        s = kind * 64 + HEAD_SIZE * h
        t0, t1 = s // 128, (s + HEAD_SIZE - 1) // 128 + 1
        win = slice(t0 * 128, t1 * 128)
        lane = lax.broadcasted_iota(jnp.int32, (1, (t1 - t0) * 128), 1) + t0 * 128
        ours = jnp.logical_and(lane >= s, lane < s + HEAD_SIZE).astype(F32).astype(BF)
        qh, kh, vh, uh = (a[:, win] * ours for a in (q, k, v, u))
        sc = jnp.where(allowed, nt(qh, kh) * factor, NEG)
        e = jnp.exp(sc - jnp.max(sc, -1, keepdims=True))
        p = e * (1.0 / jnp.sum(e, -1, keepdims=True))
        pb = p.astype(BF)
        gp = nt(uh, vh)
        pg = p * gp
        gs = ((pg - p * jnp.sum(pg, -1, keepdims=True)) * factor).astype(BF)
        res = (nn(gs, kh), tn(gs, qh), tn(pb, uh), nn(pb, vh))
        for j, r in enumerate(res):
            for t in range(t0, t1):
                part = r[:, (t - t0) * 128 : (t - t0 + 1) * 128]
                sums[j][t] = part if sums[j][t] is None else sums[j][t] + part
        for t in range(5):
            if s < (t + 1) * 128 <= s + HEAD_SIZE or (h == 7 and t == 4):
                for j in range(4):
                    g4[j // 2, j % 2, :, t * 128 : (t + 1) * 128] = sums[j][t].astype(BF)
    gh = nt(g4[0, 0], w[0]) + nt(g4[0, 1], w[1]) + nt(g4[1, 0], w[2])
    if kind == 0:
        outs[2][...] = g4[1, 1]
        outs[3][...] = gh
    else:
        outs[2][:, :HALF] = g4[1, 1]
        outs[2][:, HALF:] = gh.astype(BF)
    keep_ref[...] = g4[core]
    send_ref[...] = g4[1 - core]
    if kind == 0:
        for c in backs:
            c.wait()


def attend_call(kind, coord, mask, hid, cot, w_qkv, w_out, edge, pieces, plan):
    s = jax.ShapeDtypeStruct
    both = s((2, TOK, HALF), BF)
    if kind == 0:
        outs, specs = (s((TOK, HALF), BF), s((TOK, D), F32), s((D, D), BF), s((3, D, 128), BF)), (VM, VM, HBM, HBM)
    else:
        outs, specs = (s((TOK, HALF + D), BF), s((D, TOK), BF), s((TOK, D), BF)), (VM,) * 3
    return pl.pallas_call(
        lambda *refs: attend_kernel(kind, plan, len(pieces), *refs),
        out_shape=(both, both) + outs,
        in_specs=[SM] + [VM] * 3 + [HBM] * (3 + len(pieces)),
        out_specs=(VM, VM) + specs,
        scratch_shapes=[
            pltpu.VMEM((3, D, HALF), BF),
            pltpu.VMEM((D, D), BF),
            pltpu.VMEM((2, 2, TOK, HALF), BF),
            pltpu.SemaphoreType.DMA((len(plan), 2)),
            pltpu.SemaphoreType.DMA((7,)),
        ],
        compiler_params=PARAMS,
        cost_estimate=pl.CostEstimate(flops=6 * 10**9, bytes_accessed=16 * 10**6, transcendentals=10**6),
        name=("attend_space", "attend_time")[kind],
    )(coord, mask, hid, cot, w_qkv, w_out, edge, *pieces)


SHIP0 = ((0, (1, 2)), (0, (0, 3)), (1, (3, 2)), (1, (0, 1)))
SHIP1 = ((1, (0, 1)), (1, (2, 3)), (0, (0, 1, 2, 3)))


def weight_kernel(coord, hft, hpt, hft2, hpt2, cf, cp, cf2, cp2, kf, kp, rf, rp, *refs):
    outs, (a0, a1, sem) = refs[:7], refs[7:]
    core, zl, y = coord[0], coord[1], coord[2]

    def by_hidden(x, out):
        tiles = [((0, 256), None), ((256, 512), None), ((512, 640), (0, 128)), (None, (128, 384)), (None, (384, 640))]
        at = 0
        for f, p in tiles:
            parts = []
            if f is not None:
                sl = slice(*f)
                parts += [nn(hft[...], kf[x, :, sl]), nn(hft2[...], rf[x, :, sl])]
            if p is not None:
                sl = slice(*p)
                parts += [nn(hpt[...], kp[x, :, sl]), nn(hpt2[...], rp[x, :, sl])]
            total = sum(parts[1:], parts[0])
            out[:, at : at + total.shape[1]] = total.astype(BF)
            at += total.shape[1]

    def by_attended(x, out):
        for c in range(0, D, 384):
            sl = slice(c, c + 384)
            f = tn(kf[x], cf[:, sl]) + tn(rf[x], cf2[:, sl])
            p = tn(kp[x], cp[:, sl]) + tn(rp[x], cp2[:, sl])
            out[0:512, sl] = f[:512].astype(BF)
            out[512:640, sl] = (f[512:] + p[:128]).astype(BF)
            out[640:1152, sl] = p[128:].astype(BF)

    def ship(scratch, ships, refs, n):
        copies = []
        for r, ((a, order), out) in enumerate(zip(ships, refs)):
            for i, j in enumerate(order):
                rep = lax.rem(zl + a, 2) * 4 + jnp.bitwise_xor(y, j)
                rows = pl.ds(pl.multiple_of(rep * ROWS, 16), ROWS)
                c = pltpu.make_async_copy(scratch.at[rows, :], out.at[i], sem.at[n, r, i])
                c.start()
                copies.append(c)
        return copies

    by_hidden(0, a0)
    c0 = ship(a0, SHIP0, outs[:4], 0)

    @pl.when(core == 0)
    def _():
        by_hidden(1, a1)

    @pl.when(core == 1)
    def _():
        by_attended(1, a1)

    c1 = ship(a1, SHIP1, outs[4:], 1)
    for c in c0 + c1:
        c.wait()


def weight_call(coord, *args):
    outs = tuple(jax.ShapeDtypeStruct((len(o), ROWS, D), BF) for _, o in SHIP0 + SHIP1)
    return pl.pallas_call(
        weight_kernel,
        out_shape=outs,
        in_specs=[SM] + [VM] * len(args),
        out_specs=(HBM,) * len(outs),
        scratch_shapes=[pltpu.VMEM((D, D), BF), pltpu.VMEM((D, D), BF), pltpu.SemaphoreType.DMA((2, 4, 4))],
        compiler_params=PARAMS,
        cost_estimate=pl.CostEstimate(flops=6 * 10**9, bytes_accessed=16 * 10**6, transcendentals=0),
        name="weight_grads",
    )(coord, *args)


def finish_kernel(lat_ref, cot_ref, att_ref, ghf_ref, back_ref, wo_ref, out_ref, gl_ref):
    lat = lat_ref[...]
    mixed = nn(att_ref[...], wo_ref[0:HALF, :]) + nn(back_ref[:, :HALF], wo_ref[TOFF:D, :])
    out_ref[...] = (lat.astype(F32) + mixed).astype(BF)
    normed, r = normalize(lat)
    gh = ghf_ref[...] + back_ref[:, HALF:].astype(F32)
    mean = jnp.mean(gh, -1, keepdims=True)
    dot = jnp.mean(gh * normed, -1, keepdims=True)
    gl_ref[...] = (cot_ref[...].astype(F32) + r * (gh - mean - normed * dot)).astype(BF)


def finish_call(*args):
    s = jax.ShapeDtypeStruct((TOK, D), BF)
    return pl.pallas_call(
        finish_kernel,
        out_shape=(s, s),
        in_specs=[VM] * 6,
        out_specs=(VM, VM),
        compiler_params=PARAMS,
        cost_estimate=pl.CostEstimate(flops=10**9, bytes_accessed=8 * 10**6, transcendentals=0),
        name="finish",
    )(*args)


def pairs(move):
    out = []
    for x in range(4):
        for z in range(8):
            for c in range(2):
                for y in range(4):
                    to = move(x, y, z, c)
                    spot = []
                    for xx, yy, zz, cc in ((x, y, z, c), (to[0] % 4, to[1] % 4, to[2] % 8, to[3])):
                        spot.append(((xx * 4 + zz // 2) * 2 + cc) * 8 + (zz % 2) * 4 + yy)
                    out.append(tuple(spot))
    return out


CORE = pairs(lambda x, y, z, c: (x, y, z, 1 - c))
XP = [pairs(lambda x, y, z, c, d=d: (x + d, y, z, c)) for d in range(4)]
YP = [pairs(lambda x, y, z, c, d=d: (x, y + d, z, c)) for d in range(4)]
ZP = [pairs(lambda x, y, z, c, d=d: (x, y, z + d, c)) for d in range(8)]
Y1 = pairs(lambda x, y, z, c: (x, y ^ 1, z, c))
Y3 = pairs(lambda x, y, z, c: (x, y ^ 3, z, c))
Z1 = pairs(lambda x, y, z, c: (x, y, z ^ 1, c))
Z1B = pairs(lambda x, y, z, c: (x, y, (z + 1 if z % 2 else z - 1), c))


def move(a, p):
    return lax.ppermute(a, AXES, p)


def add(*terms):
    total = terms[0].astype(F32)
    for t in terms[1:]:
        total = total + t.astype(F32)
    return total


def gather_weights(coord, w_qkv, w_out, early):
    e, g = pack_call(coord, w_qkv, w_out)
    e_pieces, e_plan, g_pieces, g_plan = [], [], [], []

    def note(pieces, plan, array, parts):
        for other in (False, True):
            i = len(pieces)
            pieces.append(move(array, CORE) if other else array)
            for n, (name, dz, dy) in enumerate(parts):
                plan.append((lambda r, i=i, n=n: r[i].at[n], name, other, dz, dy))

    up, down = move(e, YP[1]), move(e, YP[3])
    z0, z1 = move(e[0], ZP[1]), move(e[1], ZP[7])
    gz = move(g, ZP[1])
    lat_cot, *early = early
    z0, z1, lat_cot = lax.optimization_barrier((z0, z1, lat_cot))
    pos = lax.all_to_all(lat_cot, "tm", split_axis=0, concat_axis=0, tiled=True).reshape(TOK, 2 * D)
    z = jnp.stack([z0, z1])
    zup, zdown = move(z, YP[1]), move(z, YP[3])
    gg = jnp.stack([g, gz])
    g_up, g_down, g_two = move(gg, YP[1]), move(gg, YP[3]), move(gg, YP[2])
    up, down, *early = lax.optimization_barrier((up, down, *early))
    two_up = move(jnp.stack([up[0], zup[0]]), YP[1])
    two_down = move(jnp.stack([down[1], zdown[1]]), YP[3])
    for array, dz, dy in ((z, 1, 0), (up, 0, 3), (down, 0, 1), (zup, 1, 3), (zdown, 1, 1)):
        note(e_pieces, e_plan, array, (("e0", dz, dy), ("e1", dz, dy)))
    note(e_pieces, e_plan, two_up, (("e0", 0, 2), ("e0", 1, 2)))
    note(e_pieces, e_plan, two_down, (("e1", 0, 2), ("e1", 1, 2)))
    note(g_pieces, g_plan, gz[None], (("g", 1, 0),))
    for array, dy in ((g_up, 3), (g_down, 1), (g_two, 2)):
        note(g_pieces, g_plan, array, (("g", 0, dy), ("g", 1, dy)))
    return (e_pieces, e_plan), (g_pieces, g_plan), pos, early


def all_sum(own):
    x = lax.axis_index("tm") // 8
    parts = own.reshape(4, 72, D)

    def part(i):
        return lax.dynamic_index_in_dim(parts, i % 4, 0, keepdims=False)

    got = [move(part(x + d), XP[d]) for d in (1, 2, 3)]
    mine = add(part(x), *got).astype(BF)
    two, four, six = (move(mine, ZP[d]) for d in (2, 4, 6))
    row = (add(mine, four) + add(two, six)).astype(BF)
    ring = jnp.stack([row] + [move(row, XP[d]) for d in (1, 2, 3)])
    return jnp.take(ring, (x - jnp.arange(4)) % 4, axis=0).reshape(2, ROWS, D)


def reduce_out0(s0a, k0a, s0b, k0b):
    ga, gb = move(s0a, Y1), move(s0b, Y3)
    ka, kb = add(k0a, ga).astype(BF), add(k0b, gb).astype(BF)
    ga, gb = move(ka[1], Y3), move(kb[1], Y1)
    ours, theirs = add(ka[0], ga), add(kb[0], gb).astype(BF)
    return add(ours, move(theirs, Z1)).astype(BF)


def reduce_out1(sa, sb, keep):
    ga, gb = move(sa, Z1), move(sb, Z1B)
    b = [add(keep[0], ga[0]), add(keep[1], ga[1]), add(keep[2], gb[0]), add(keep[3], gb[1])]
    b = [t.astype(BF) for t in b]
    top, low = [t[:72] for t in b], [t[72:] for t in b]
    gt = move(jnp.stack([top[1], top[2]]), Y1)
    gl = move(jnp.stack([low[3], low[2]]), Y3)
    t0, t3 = add(top[0], gt[0]).astype(BF), add(top[3], gt[1]).astype(BF)
    l0, l1 = add(low[0], gl[0]).astype(BF), add(low[1], gl[1]).astype(BF)
    gt, gl = move(t3, Y3), move(l1, Y1)
    return jnp.concatenate([add(t0, gt), add(l0, gl)]).astype(BF)


def local(latents, cotangent, w_qkv, w_out, tile_pattern):
    tm, rep = lax.axis_index("tm"), lax.axis_index("replica")
    core, zl, y = tm % 2, rep // 4, rep % 4
    coord = jnp.stack([core, zl, y]).astype(jnp.int32)
    lat, cot = latents.reshape(TOK, D), cotangent.reshape(TOK, D)
    lat_cot = jnp.concatenate([lat, cot], 1).reshape(32, 8, 2 * D)
    early = (lat_cot, *norm_call(tile_pattern, lat), move(cot, CORE))
    e_part, g_part, pos, early = gather_weights(coord, w_qkv, w_out, early)
    hf, hft, mask, cf2 = early

    kf, sf, att, ghf, wo, edge = attend_call(0, coord, mask, hf, cot, w_qkv, w_out, w_out, *e_part)
    rf, hft2 = move(sf, CORE), move(hft, CORE)
    kp, sp, back, hpt, cp = attend_call(1, coord, mask, pos, cot, w_qkv, wo, edge, *g_part)
    sp, rf, hft2 = lax.optimization_barrier((sp, rf, hft2))
    rp, hpt2, cp2 = move(sp, CORE), move(hpt, CORE), move(cp, CORE)
    back = lax.all_to_all(
        back.reshape(32, 8, HALF + D), "tm", split_axis=0, concat_axis=0, tiled=True
    ).reshape(TOK, HALF + D)
    w = weight_call(coord, hft, hpt, hft2, hpt2, cot, cp, cf2, cp2, kf, kp, rf, rp)
    w0, (*w1, back) = w[:4], lax.optimization_barrier((*w[4:], back))
    own = jnp.concatenate([reduce_out0(*w0), reduce_out1(*w1)])
    result, grad_input = finish_call(lat, cot, att, ghf, back, wo)
    total = all_sum(own)
    other = move(total, CORE)
    factor = 1.0 / math.sqrt(65536)
    first = core == 0
    q, k = (jnp.where(first, total[i], other[i]) for i in range(2))
    v, o = (jnp.where(first, other[i], total[i]) for i in range(2))
    dw_qkv = jnp.concatenate([q, k, v], 1).astype(F32) * factor
    dw_out = o.astype(F32) * factor
    return result.reshape(1, 1, TOK, D), grad_input.reshape(1, 1, TOK, D), dw_qkv, dw_out


def solution(mesh):
    tokens, rows = P("replica", "tm", None, None), P("replica", None)
    return jax.shard_map(
        local,
        mesh=mesh,
        in_specs=(tokens, tokens, rows, rows, P()),
        out_specs=(tokens, tokens, rows, rows),
        check_vma=False,
    )
```

```python
import math

import jax
import jax.numpy as jnp
from jax import lax
from jax.experimental import pallas as pl
from jax.experimental.pallas import tpu as pltpu
from jax.sharding import PartitionSpec as P

HEADS = 16
HEAD_SIZE = 72
SPATIAL_HEADS = 8
TOK = 256
D = 1152
HALF = 640
TOFF = 512
ROWS = 144
BF = jnp.bfloat16
F32 = jnp.float32
NEG = -1e30
VMEM_LIMIT = 60 * 1024 * 1024
AXES = ("tm", "replica")
HBM = pl.BlockSpec(memory_space=pl.ANY)
VM = pl.BlockSpec(memory_space=pltpu.VMEM)
SM = pl.BlockSpec(memory_space=pltpu.SMEM)
PARAMS = pltpu.CompilerParams(vmem_limit_bytes=VMEM_LIMIT)


def nn(a, b):
    return lax.dot_general(a, b, (((1,), (0,)), ((), ())), preferred_element_type=F32)


def nt(a, b):
    return lax.dot_general(a, b, (((1,), (1,)), ((), ())), preferred_element_type=F32)


def tn(a, b):
    return lax.dot_general(a, b, (((0,), (0,)), ((), ())), preferred_element_type=F32)


def normalize(x):
    x = x.astype(F32)
    centred = x - jnp.mean(x, -1, keepdims=True)
    r = lax.rsqrt(jnp.mean(centred * centred, -1, keepdims=True) + 1e-06)
    return centred * r, r


def pack_kernel(coord, wqkv_ref, wout_ref, e_ref, g_ref, z0_ref, z1_ref):
    q, k, v = 0, D, 2 * D

    @pl.when(coord[0] == 0)
    def _():
        e_ref[0, :, 0:640] = wqkv_ref[:, q : q + 640]
        e_ref[0, :, 640:768] = wqkv_ref[:, k : k + 128]
        e_ref[1, :, 0:512] = wqkv_ref[:, k + 128 : k + 640]
        e_ref[1, :, 512:768] = wqkv_ref[:, v : v + 256]
        g_ref[:, 0:512] = wqkv_ref[:, q + 640 : q + D]
        g_ref[:, 512:768] = wqkv_ref[:, v + 640 : v + 896]

    @pl.when(coord[0] == 1)
    def _():
        e_ref[0, :, 0:384] = wqkv_ref[:, v + 256 : v + 640]
        e_ref[0, :, 384:768] = wout_ref[:, 0:384]
        e_ref[1, :, :] = wout_ref[:, 384:]
        g_ref[:, 0:512] = wqkv_ref[:, k + 640 : k + D]
        g_ref[:, 512:768] = wqkv_ref[:, v + 896 : v + D]

    for n, z_ref in enumerate((z0_ref, z1_ref)):
        z_ref[:, 0:768] = e_ref[n]
        z_ref[:, 768:] = g_ref[:, 384 * n : 384 * (n + 1)]


def pack_call(coord, w_qkv, w_out):
    s = jax.ShapeDtypeStruct
    return pl.pallas_call(
        pack_kernel,
        out_shape=(s((2, ROWS, 768), BF), s((ROWS, 768), BF)) + (s((ROWS, D), BF),) * 2,
        in_specs=[SM, VM, VM],
        out_specs=(VM,) * 4,
        compiler_params=PARAMS,
        cost_estimate=pl.CostEstimate(flops=0, bytes_accessed=2 * 10**6, transcendentals=0),
        name="pack",
    )(coord, w_qkv, w_out)


def norm_kernel(tile_ref, src_ref, h_ref, ht_ref, mask_ref):
    n, _ = normalize(src_ref[...])
    h_ref[...] = n.astype(BF)
    ht_ref[...] = n.T.astype(BF)
    row = lax.broadcasted_iota(jnp.int32, (TOK, TOK), 0)
    col = lax.broadcasted_iota(jnp.int32, (TOK, TOK), 1)
    mask_ref[1] = (row % 8 == col % 8).astype(F32)
    col = lax.broadcasted_iota(jnp.int32, (64, TOK), 1) // 64
    for i in range(4):
        line = jnp.zeros((64, TOK), F32)
        for j in range(4):
            line = jnp.where(col == j, (tile_ref[j, i] == 1).astype(F32), line)
        mask_ref[0, 64 * i : 64 * (i + 1), :] = line


def norm_call(tile_pattern, src):
    s = jax.ShapeDtypeStruct
    outs = (s((TOK, D), BF), s((D, TOK), BF), s((2, TOK, TOK), F32))
    return pl.pallas_call(
        norm_kernel,
        out_shape=outs,
        in_specs=[SM, VM],
        out_specs=(VM,) * len(outs),
        compiler_params=PARAMS,
        cost_estimate=pl.CostEstimate(flops=10**8, bytes_accessed=2 * 10**6, transcendentals=0),
        name="norm",
    )(tile_pattern, src)


SPREAD = {
    "e0": (((0, 640, 0, 0), (640, 768, 1, 0)), ((0, 384, 2, 256), (384, 768, 3, 0))),
    "e1": (((0, 512, 1, 128), (512, 768, 2, 0)), ((0, 768, 3, 384),)),
    "g": (((0, 512, 0, 128), (512, 768, 2, 128)), ((0, 512, 1, 128), (512, 768, 2, 384))),
}


def load_weights(plan, pieces, w, wo, sem, coord):
    core, zl, y = coord[0], coord[1], coord[2]
    waits = []
    for n, (view, name, other, dz, dy) in enumerate(plan):
        rep = lax.rem(zl + dz, 2) * 4 + lax.rem(y + dy, 4)
        rows = pl.ds(pl.multiple_of(rep * ROWS, 16), ROWS)
        src = view(pieces)
        owner = 1 - core if other else core
        for c, spread in enumerate(SPREAD[name]):
            copies = []
            for k, (c0, c1, quarter, to) in enumerate(spread):
                dst = wo.at[rows, to : to + c1 - c0] if quarter == 3 else w.at[quarter, rows, to : to + c1 - c0]
                copies.append(pltpu.make_async_copy(src.at[:, c0:c1], dst, sem.at[n, k]))

            @pl.when(owner == c)
            def _(copies=copies):
                for d in copies:
                    d.start()

            waits.append((owner == c, copies))

    def wait():
        for when, copies in waits:

            @pl.when(when)
            def _(copies=copies):
                for d in copies:
                    d.wait()

    return wait


def attend_kernel(kind, plan, n_piece, *refs):
    coord, mask_ref, hid_ref, cot_ref, wqkv_ref, wout_ref, edge_ref = refs[:7]
    pieces = refs[7 : 7 + n_piece]
    outs = refs[7 + n_piece : -5]
    w, wo, g4, sem, own_sem = refs[-5:]
    keep_ref, send_ref = outs[:2]
    core, zl, y = coord[0], coord[1], coord[2]
    cols = slice(kind * TOFF, kind * TOFF + HALF)
    wait = load_weights(plan, pieces, w, wo, sem, coord)
    rows = pl.ds(pl.multiple_of((zl * 4 + y) * ROWS, 16), ROWS)
    copies = []
    for t in range(3):
        if kind == 0:
            src, dst = wqkv_ref.at[:, t * D : t * D + HALF], w.at[t, rows, :]
        else:
            src, dst = wqkv_ref.at[:, t * D + HALF : (t + 1) * D], w.at[t, rows, 128:]
            copies.append(pltpu.make_async_copy(edge_ref.at[t], w.at[t, :, 0:128], own_sem.at[4 + t]))
        copies.append(pltpu.make_async_copy(src, dst, own_sem.at[t]))
    if kind == 0:
        copies.append(pltpu.make_async_copy(wout_ref, wo.at[rows, :], own_sem.at[3]))
    else:
        copies.append(pltpu.make_async_copy(wout_ref, wo, own_sem.at[3]))
    for c in copies:
        c.start()
    if kind == 1:
        normed, _ = normalize(hid_ref[:, :D])
        hid = normed.astype(BF)
        cot = hid_ref[:, D:]
        outs[3][...] = normed.T.astype(BF)
        outs[4][...] = cot
    else:
        hid, cot = hid_ref[...], cot_ref[...]
    for c in copies:
        c.wait()
    wait()
    if kind == 0:
        backs = [pltpu.make_async_copy(wo, outs[4], own_sem.at[3])]
        for t in range(3):
            backs.append(pltpu.make_async_copy(w.at[t, :, TOFF:HALF], outs[5].at[t], own_sem.at[t]))
        for c in backs:
            c.start()
    factor = 1.0 / math.sqrt(HEAD_SIZE)
    q = nn(hid, w[0]).astype(BF)
    k = nn(hid, w[1]).astype(BF)
    v = nn(hid, w[2]).astype(BF)
    u = nt(cot, wo[cols, :]).astype(BF)
    allowed = mask_ref[kind] > 0
    sums = [[None] * 5 for _ in range(4)]
    for h in range(8):
        s = kind * 64 + HEAD_SIZE * h
        t0, t1 = s // 128, (s + HEAD_SIZE - 1) // 128 + 1
        win = slice(t0 * 128, t1 * 128)
        lane = lax.broadcasted_iota(jnp.int32, (1, (t1 - t0) * 128), 1) + t0 * 128
        ours = jnp.logical_and(lane >= s, lane < s + HEAD_SIZE).astype(F32).astype(BF)
        qh, kh, vh, uh = (a[:, win] * ours for a in (q, k, v, u))
        sc = jnp.where(allowed, nt(kh, qh) * factor, NEG)
        e = jnp.exp(sc - jnp.max(sc, 0, keepdims=True))
        p = e * (1.0 / jnp.sum(e, 0, keepdims=True))
        pb = p.astype(BF)
        gp = nt(vh, uh)
        pg = p * gp
        gs = ((pg - p * jnp.sum(pg, 0, keepdims=True)) * factor).astype(BF)
        res = (tn(gs, kh), nn(gs, qh), nn(pb, uh), tn(pb, vh))
        for j, r in enumerate(res):
            for t in range(t0, t1):
                part = r[:, (t - t0) * 128 : (t - t0 + 1) * 128]
                sums[j][t] = part if sums[j][t] is None else sums[j][t] + part
        for t in range(5):
            if s < (t + 1) * 128 <= s + HEAD_SIZE or (h == 7 and t == 4):
                for j in range(4):
                    g4[j // 2, j % 2, :, t * 128 : (t + 1) * 128] = sums[j][t].astype(BF)
    gh = nt(g4[0, 0], w[0]) + nt(g4[0, 1], w[1]) + nt(g4[1, 0], w[2])
    if kind == 0:
        outs[2][...] = g4[1, 1]
        outs[3][...] = gh
    else:
        outs[2][:, :HALF] = g4[1, 1]
        outs[2][:, HALF:] = gh.astype(BF)
    keep_ref[...] = g4[core]
    send_ref[...] = g4[1 - core]
    if kind == 0:
        for c in backs:
            c.wait()


def attend_call(kind, coord, mask, hid, cot, w_qkv, w_out, edge, pieces, plan):
    s = jax.ShapeDtypeStruct
    both = s((2, TOK, HALF), BF)
    if kind == 0:
        outs, specs = (s((TOK, HALF), BF), s((TOK, D), F32), s((D, D), BF), s((3, D, 128), BF)), (VM, VM, HBM, HBM)
    else:
        outs, specs = (s((TOK, HALF + D), BF), s((D, TOK), BF), s((TOK, D), BF)), (VM,) * 3
    return pl.pallas_call(
        lambda *refs: attend_kernel(kind, plan, len(pieces), *refs),
        out_shape=(both, both) + outs,
        in_specs=[SM] + [VM] * 3 + [HBM] * (3 + len(pieces)),
        out_specs=(VM, VM) + specs,
        scratch_shapes=[
            pltpu.VMEM((3, D, HALF), BF),
            pltpu.VMEM((D, D), BF),
            pltpu.VMEM((2, 2, TOK, HALF), BF),
            pltpu.SemaphoreType.DMA((len(plan), 2)),
            pltpu.SemaphoreType.DMA((7,)),
        ],
        compiler_params=PARAMS,
        cost_estimate=pl.CostEstimate(flops=6 * 10**9, bytes_accessed=16 * 10**6, transcendentals=10**6),
        name=("attend_space", "attend_time")[kind],
    )(coord, mask, hid, cot, w_qkv, w_out, edge, *pieces)


SHIP0 = ((0, (1, 2)), (0, (0, 3)), (1, (3, 2)), (1, (0, 1)))
SHIP1 = ((1, (0, 1)), (1, (2, 3)), (0, (0, 1, 2, 3)))


def weight_kernel(index, coord, hft, hpt, hft2, hpt2, cf, cp, cf2, cp2, kf, kp, rf, rp, *refs):
    outs, (held, sem) = refs[:-2], refs[-2:]
    core, zl, y = coord[0], coord[1], coord[2]

    def by_hidden(x, out):
        tiles = [((0, 256), None), ((256, 512), None), ((512, 640), (0, 128)), (None, (128, 384)), (None, (384, 640))]
        at = 0
        for f, p in tiles:
            parts = []
            if f is not None:
                sl = slice(*f)
                parts += [nn(hft[...], kf[x, :, sl]), nn(hft2[...], rf[x, :, sl])]
            if p is not None:
                sl = slice(*p)
                parts += [nn(hpt[...], kp[x, :, sl]), nn(hpt2[...], rp[x, :, sl])]
            total = sum(parts[1:], parts[0])
            out[:, at : at + total.shape[1]] = total.astype(BF)
            at += total.shape[1]

    def by_attended(x, out):
        for c in range(0, D, 384):
            sl = slice(c, c + 384)
            f = tn(kf[x], cf[:, sl]) + tn(rf[x], cf2[:, sl])
            p = tn(kp[x], cp[:, sl]) + tn(rp[x], cp2[:, sl])
            out[0:512, sl] = f[:512].astype(BF)
            out[512:640, sl] = (f[512:] + p[:128]).astype(BF)
            out[640:1152, sl] = p[128:].astype(BF)

    if index == 0:
        by_hidden(0, held)
    else:

        @pl.when(core == 0)
        def _():
            by_hidden(1, held)

        @pl.when(core == 1)
        def _():
            by_attended(1, held)

    copies = []
    for r, ((a, order), out) in enumerate(zip((SHIP0, SHIP1)[index], outs)):
        for i, j in enumerate(order):
            rep = lax.rem(zl + a, 2) * 4 + jnp.bitwise_xor(y, j)
            rows = pl.ds(pl.multiple_of(rep * ROWS, 16), ROWS)
            c = pltpu.make_async_copy(held.at[rows, :], out.at[i], sem.at[r, i])
            c.start()
            copies.append(c)
    for c in copies:
        c.wait()


def weight_call(index, coord, *args):
    outs = tuple(jax.ShapeDtypeStruct((len(o), ROWS, D), BF) for _, o in (SHIP0, SHIP1)[index])
    cot = HBM if index == 0 else VM
    return pl.pallas_call(
        lambda *refs: weight_kernel(index, *refs),
        out_shape=outs,
        in_specs=[SM] + [VM] * 4 + [cot] * 4 + [VM] * 4,
        out_specs=(HBM,) * len(outs),
        scratch_shapes=[pltpu.VMEM((D, D), BF), pltpu.SemaphoreType.DMA((4, 4))],
        compiler_params=PARAMS,
        cost_estimate=pl.CostEstimate(flops=3 * 10**9, bytes_accessed=8 * 10**6, transcendentals=0),
        name="weight_grads",
    )(coord, *args)


def finish_kernel(lat_ref, cot_ref, att_ref, ghf_ref, back_ref, wo_ref, out_ref, gl_ref):
    lat = lat_ref[...]
    mixed = nn(att_ref[...], wo_ref[0:HALF, :]) + nn(back_ref[:, :HALF], wo_ref[TOFF:D, :])
    out_ref[...] = (lat.astype(F32) + mixed).astype(BF)
    normed, r = normalize(lat)
    gh = ghf_ref[...] + back_ref[:, HALF:].astype(F32)
    mean = jnp.mean(gh, -1, keepdims=True)
    dot = jnp.mean(gh * normed, -1, keepdims=True)
    gl_ref[...] = (cot_ref[...].astype(F32) + r * (gh - mean - normed * dot)).astype(BF)


def finish_call(*args):
    s = jax.ShapeDtypeStruct((TOK, D), BF)
    return pl.pallas_call(
        finish_kernel,
        out_shape=(s, s),
        in_specs=[VM] * 6,
        out_specs=(VM, VM),
        compiler_params=PARAMS,
        cost_estimate=pl.CostEstimate(flops=10**9, bytes_accessed=8 * 10**6, transcendentals=0),
        name="finish",
    )(*args)


def pairs(move):
    out = []
    for x in range(4):
        for z in range(8):
            for c in range(2):
                for y in range(4):
                    to = move(x, y, z, c)
                    spot = []
                    for xx, yy, zz, cc in ((x, y, z, c), (to[0] % 4, to[1] % 4, to[2] % 8, to[3])):
                        spot.append(((xx * 4 + zz // 2) * 2 + cc) * 8 + (zz % 2) * 4 + yy)
                    out.append(tuple(spot))
    return out


CORE = pairs(lambda x, y, z, c: (x, y, z, 1 - c))
XP = [pairs(lambda x, y, z, c, d=d: (x + d, y, z, c)) for d in range(4)]
YP = [pairs(lambda x, y, z, c, d=d: (x, y + d, z, c)) for d in range(4)]
ZP = [pairs(lambda x, y, z, c, d=d: (x, y, z + d, c)) for d in range(8)]
Y1 = pairs(lambda x, y, z, c: (x, y ^ 1, z, c))
Y3 = pairs(lambda x, y, z, c: (x, y ^ 3, z, c))
Z1 = pairs(lambda x, y, z, c: (x, y, z ^ 1, c))
Z1B = pairs(lambda x, y, z, c: (x, y, (z + 1 if z % 2 else z - 1), c))


def move(a, p):
    return lax.ppermute(a, AXES, p)


def add(*terms):
    total = terms[0].astype(F32)
    for t in terms[1:]:
        total = total + t.astype(F32)
    return total


def gather_weights(coord, w_qkv, w_out, early):
    e, g, z0, z1 = pack_call(coord, w_qkv, w_out)
    e_pieces, e_plan, g_pieces, g_plan = [], [], [], []

    def note(pieces, plan, array, parts):
        for other in (False, True):
            i = len(pieces)
            pieces.append(move(array, CORE) if other else array)
            for n, (name, dz, dy) in enumerate(parts):
                plan.append((lambda r, i=i, n=n: r[i].at[n], name, other, dz, dy))

    up, down = move(e, YP[1]), move(e, YP[3])
    z0, z1 = move(z0, ZP[1]), move(z1, ZP[7])
    z = jnp.stack([z0[:, :768], z1[:, :768]])
    gz = jnp.concatenate([z0[:, 768:], z1[:, 768:]], 1)
    zup, zdown = move(z, YP[1]), move(z, YP[3])
    up, down, *early = lax.optimization_barrier((up, down, *early))
    lat_cot, *early = early
    pos = lax.all_to_all(lat_cot, "tm", split_axis=0, concat_axis=0, tiled=True).reshape(TOK, 2 * D)
    relays = [move(up[0], YP[1]), move(down[1], YP[3]), move(zup[0], YP[1]), move(zdown[1], YP[3])]
    *relays, g, gz = lax.optimization_barrier((*relays, g, gz))
    gg = jnp.stack([g, gz])
    g_all = (gz[None], move(gg, YP[1]), move(gg, YP[3]), move(gg, YP[2]))
    for array, dz, dy in ((z, 1, 0), (up, 0, 3), (down, 0, 1), (zup, 1, 3), (zdown, 1, 1)):
        note(e_pieces, e_plan, array, (("e0", dz, dy), ("e1", dz, dy)))
    for n, array in enumerate(relays):
        note(e_pieces, e_plan, array[None], ((("e0", "e1")[n % 2], n // 2, 2),))

    def second(after):
        after, *arrays = lax.optimization_barrier((after, *g_all))
        note(g_pieces, g_plan, arrays[0], (("g", 1, 0),))
        for array, dy in zip(arrays[1:], (3, 1, 2)):
            note(g_pieces, g_plan, array, (("g", 0, dy), ("g", 1, dy)))
        return after, g_pieces, g_plan

    return (e_pieces, e_plan), second, pos, early


def all_sum(own):
    x = lax.axis_index("tm") // 8
    parts = own.reshape(4, 72, D)

    def part(i):
        return lax.dynamic_index_in_dim(parts, i % 4, 0, keepdims=False)

    got = [move(part(x + d), XP[d]) for d in (1, 2, 3)]
    mine = add(part(x), *got).astype(BF)
    two, four, six = (move(mine, ZP[d]) for d in (2, 4, 6))
    row = (add(mine, four) + add(two, six)).astype(BF)
    ring = jnp.stack([row] + [move(row, XP[d]) for d in (1, 2, 3)])
    return jnp.take(ring, (x - jnp.arange(4)) % 4, axis=0).reshape(2, ROWS, D)


def reduce_out0(s0a, k0a, s0b, k0b):
    ga, gb = move(s0a, Y1), move(s0b, Y3)
    ka, kb = add(k0a, ga).astype(BF), add(k0b, gb).astype(BF)
    ga, gb = move(ka[1], Y3), move(kb[1], Y1)
    ours, theirs = add(ka[0], ga), add(kb[0], gb).astype(BF)
    return add(ours, move(theirs, Z1)).astype(BF)


def reduce_out1(sa, sb, keep):
    ga, gb = move(sa, Z1), move(sb, Z1B)
    b = [add(keep[0], ga[0]), add(keep[1], ga[1]), add(keep[2], gb[0]), add(keep[3], gb[1])]
    b = [t.astype(BF) for t in b]
    top, low = [t[:72] for t in b], [t[72:] for t in b]
    gt = move(jnp.stack([top[1], top[2]]), Y1)
    gl = move(jnp.stack([low[3], low[2]]), Y3)
    t0, t3 = add(top[0], gt[0]).astype(BF), add(top[3], gt[1]).astype(BF)
    l0, l1 = add(low[0], gl[0]).astype(BF), add(low[1], gl[1]).astype(BF)
    gt, gl = move(t3, Y3), move(l1, Y1)
    return jnp.concatenate([add(t0, gt), add(l0, gl)]).astype(BF)


def local(latents, cotangent, w_qkv, w_out, tile_pattern):
    tm, rep = lax.axis_index("tm"), lax.axis_index("replica")
    core, zl, y = tm % 2, rep // 4, rep % 4
    coord = jnp.stack([core, zl, y]).astype(jnp.int32)
    lat, cot = latents.reshape(TOK, D), cotangent.reshape(TOK, D)
    lat_cot = jnp.concatenate([lat, cot], 1).reshape(32, 8, 2 * D)
    early = (lat_cot, *norm_call(tile_pattern, lat), move(cot, CORE))
    e_part, second, pos, early = gather_weights(coord, w_qkv, w_out, early)
    hf, hft, mask, cf2 = early

    kf, sf, att, ghf, wo, edge = attend_call(0, coord, mask, hf, cot, w_qkv, w_out, w_out, *e_part)
    edge, *g_part = second(edge)
    rf, hft2 = move(sf, CORE), move(hft, CORE)
    kp, sp, back, hpt, cp = attend_call(1, coord, mask, pos, cot, w_qkv, wo, edge, *g_part)
    sp, rf, hft2 = lax.optimization_barrier((sp, rf, hft2))
    rp, hpt2, cp2 = move(sp, CORE), move(hpt, CORE), move(cp, CORE)
    terms = (coord, hft, hpt, hft2, hpt2, cot, cp, cf2, cp2, kf, kp, rf, rp)
    w0, w1 = weight_call(0, *terms), weight_call(1, *terms)
    *w1, back = lax.optimization_barrier((*w1, back))
    back = lax.all_to_all(
        back.reshape(32, 8, HALF + D), "tm", split_axis=0, concat_axis=0, tiled=True
    ).reshape(TOK, HALF + D)
    own = jnp.concatenate([reduce_out0(*w0), reduce_out1(*w1)])
    own, back = lax.optimization_barrier((own, back))
    result, grad_input = finish_call(lat, cot, att, ghf, back, wo)
    total = all_sum(own)
    other = move(total, CORE)
    factor = 1.0 / math.sqrt(65536)
    first = core == 0
    q, k = (jnp.where(first, total[i], other[i]) for i in range(2))
    v, o = (jnp.where(first, other[i], total[i]) for i in range(2))
    dw_qkv = jnp.concatenate([q, k, v], 1).astype(F32) * factor
    dw_out = o.astype(F32) * factor
    return result.reshape(1, 1, TOK, D), grad_input.reshape(1, 1, TOK, D), dw_qkv, dw_out


def solution(mesh):
    tokens, rows = P("replica", "tm", None, None), P("replica", None)
    return jax.shard_map(
        local,
        mesh=mesh,
        in_specs=(tokens, tokens, rows, rows, P()),
        out_specs=(tokens, tokens, rows, rows),
        check_vma=False,
    )
```

```python
import math

import jax
import jax.numpy as jnp
from jax import lax
from jax.experimental import pallas as pl
from jax.experimental.pallas import tpu as pltpu
from jax.sharding import PartitionSpec as P

HEADS = 16
HEAD_SIZE = 72
SPATIAL_HEADS = 8
TOK = 256
D = 1152
HALF = 640
TOFF = 512
ROWS = 144
BF = jnp.bfloat16
F32 = jnp.float32
NEG = -1e30
VMEM_LIMIT = 60 * 1024 * 1024
AXES = ("tm", "replica")
HBM = pl.BlockSpec(memory_space=pl.ANY)
VM = pl.BlockSpec(memory_space=pltpu.VMEM)
SM = pl.BlockSpec(memory_space=pltpu.SMEM)
PARAMS = pltpu.CompilerParams(vmem_limit_bytes=VMEM_LIMIT)


def nn(a, b):
    return lax.dot_general(a, b, (((1,), (0,)), ((), ())), preferred_element_type=F32)


def nt(a, b):
    return lax.dot_general(a, b, (((1,), (1,)), ((), ())), preferred_element_type=F32)


def tn(a, b):
    return lax.dot_general(a, b, (((0,), (0,)), ((), ())), preferred_element_type=F32)


def normalize(x):
    x = x.astype(F32)
    centred = x - jnp.mean(x, -1, keepdims=True)
    r = lax.rsqrt(jnp.mean(centred * centred, -1, keepdims=True) + 1e-06)
    return centred * r, r


def pack_kernel(coord, wqkv_ref, wout_ref, e_ref, g_ref, z0_ref, z1_ref):
    q, k, v = 0, D, 2 * D

    @pl.when(coord[0] == 0)
    def _():
        e_ref[0, :, 0:640] = wqkv_ref[:, q : q + 640]
        e_ref[0, :, 640:768] = wqkv_ref[:, k : k + 128]
        e_ref[1, :, 0:512] = wqkv_ref[:, k + 128 : k + 640]
        e_ref[1, :, 512:768] = wqkv_ref[:, v : v + 256]
        g_ref[:, 0:512] = wqkv_ref[:, q + 640 : q + D]
        g_ref[:, 512:768] = wqkv_ref[:, v + 640 : v + 896]

    @pl.when(coord[0] == 1)
    def _():
        e_ref[0, :, 0:384] = wqkv_ref[:, v + 256 : v + 640]
        e_ref[0, :, 384:768] = wout_ref[:, 0:384]
        e_ref[1, :, :] = wout_ref[:, 384:]
        g_ref[:, 0:512] = wqkv_ref[:, k + 640 : k + D]
        g_ref[:, 512:768] = wqkv_ref[:, v + 896 : v + D]

    for n, z_ref in enumerate((z0_ref, z1_ref)):
        z_ref[:, 0:768] = e_ref[n]
        z_ref[:, 768:] = g_ref[:, 384 * n : 384 * (n + 1)]


def pack_call(coord, w_qkv, w_out):
    s = jax.ShapeDtypeStruct
    return pl.pallas_call(
        pack_kernel,
        out_shape=(s((2, ROWS, 768), BF), s((ROWS, 768), BF)) + (s((ROWS, D), BF),) * 2,
        in_specs=[SM, VM, VM],
        out_specs=(VM,) * 4,
        compiler_params=PARAMS,
        cost_estimate=pl.CostEstimate(flops=0, bytes_accessed=2 * 10**6, transcendentals=0),
        name="pack",
    )(coord, w_qkv, w_out)


def norm_kernel(tile_ref, src_ref, h_ref, ht_ref, mask_ref):
    n, _ = normalize(src_ref[...])
    h_ref[...] = n.astype(BF)
    ht_ref[...] = n.T.astype(BF)
    row = lax.broadcasted_iota(jnp.int32, (TOK, TOK), 0)
    col = lax.broadcasted_iota(jnp.int32, (TOK, TOK), 1)
    mask_ref[1] = (row % 8 == col % 8).astype(F32)
    col = lax.broadcasted_iota(jnp.int32, (64, TOK), 1) // 64
    for i in range(4):
        line = jnp.zeros((64, TOK), F32)
        for j in range(4):
            line = jnp.where(col == j, (tile_ref[j, i] == 1).astype(F32), line)
        mask_ref[0, 64 * i : 64 * (i + 1), :] = line


def norm_call(tile_pattern, src):
    s = jax.ShapeDtypeStruct
    outs = (s((TOK, D), BF), s((D, TOK), BF), s((2, TOK, TOK), F32))
    return pl.pallas_call(
        norm_kernel,
        out_shape=outs,
        in_specs=[SM, VM],
        out_specs=(VM,) * len(outs),
        compiler_params=PARAMS,
        cost_estimate=pl.CostEstimate(flops=10**8, bytes_accessed=2 * 10**6, transcendentals=0),
        name="norm",
    )(tile_pattern, src)


SPREAD = {
    "e0": (((0, 640, 0, 0), (640, 768, 1, 0)), ((0, 384, 2, 256), (384, 768, 3, 0))),
    "e1": (((0, 512, 1, 128), (512, 768, 2, 0)), ((0, 768, 3, 384),)),
    "g": (((0, 512, 0, 128), (512, 768, 2, 128)), ((0, 512, 1, 128), (512, 768, 2, 384))),
}


def load_weights(plan, pieces, w, wo, sem, coord):
    core, zl, y = coord[0], coord[1], coord[2]
    waits = []
    for n, (view, name, other, dz, dy) in enumerate(plan):
        rep = lax.rem(zl + dz, 2) * 4 + lax.rem(y + dy, 4)
        rows = pl.ds(pl.multiple_of(rep * ROWS, 16), ROWS)
        src = view(pieces)
        owner = 1 - core if other else core
        for c, spread in enumerate(SPREAD[name]):
            copies = []
            for k, (c0, c1, quarter, to) in enumerate(spread):
                dst = wo.at[rows, to : to + c1 - c0] if quarter == 3 else w.at[quarter, rows, to : to + c1 - c0]
                copies.append(pltpu.make_async_copy(src.at[:, c0:c1], dst, sem.at[n, k]))

            @pl.when(owner == c)
            def _(copies=copies):
                for d in copies:
                    d.start()

            waits.append((owner == c, spread, copies))

    def wait(t):
        for when, spread, copies in waits:
            ours = [d for d, part in zip(copies, spread) if part[2] == t]
            if ours:

                @pl.when(when)
                def _(ours=ours):
                    for d in ours:
                        d.wait()

    return wait


def attend_kernel(kind, plan, n_piece, *refs):
    coord, mask_ref, hid_ref, cot_ref, wqkv_ref, wout_ref, edge_ref = refs[:7]
    pieces = refs[7 : 7 + n_piece]
    outs = refs[7 + n_piece : -5]
    w, wo, g4, sem, own_sem = refs[-5:]
    keep_ref, send_ref = outs[:2]
    core, zl, y = coord[0], coord[1], coord[2]
    cols = slice(kind * TOFF, kind * TOFF + HALF)
    wait = load_weights(plan, pieces, w, wo, sem, coord)
    rows = pl.ds(pl.multiple_of((zl * 4 + y) * ROWS, 16), ROWS)
    copies = [[] for _ in range(4)]
    for t in range(3):
        if kind == 0:
            src, dst = wqkv_ref.at[:, t * D : t * D + HALF], w.at[t, rows, :]
        else:
            src, dst = wqkv_ref.at[:, t * D + HALF : (t + 1) * D], w.at[t, rows, 128:]
            copies[t].append(pltpu.make_async_copy(edge_ref.at[t], w.at[t, :, 0:128], own_sem.at[4 + t]))
        copies[t].append(pltpu.make_async_copy(src, dst, own_sem.at[t]))
    if kind == 0:
        copies[3].append(pltpu.make_async_copy(wout_ref, wo.at[rows, :], own_sem.at[3]))
    else:
        copies[3].append(pltpu.make_async_copy(wout_ref, wo, own_sem.at[3]))
    for c in sum(copies, []):
        c.start()

    def ready(t):
        for c in copies[t]:
            c.wait()
        wait(t)

    if kind == 1:
        normed, _ = normalize(hid_ref[:, :D])
        hid = normed.astype(BF)
        cot = hid_ref[:, D:]
        outs[3][...] = normed.T.astype(BF)
        normed, _ = normalize(cot_ref[:, :D])
        outs[4][...] = normed.T.astype(BF)
    else:
        hid, cot = hid_ref[...], cot_ref[...]
    factor = 1.0 / math.sqrt(HEAD_SIZE)
    ready(0)
    q = nn(hid, w[0]).astype(BF)
    ready(1)
    k = nn(hid, w[1]).astype(BF)
    ready(2)
    v = nn(hid, w[2]).astype(BF)
    ready(3)
    u = nt(cot, wo[cols, :]).astype(BF)
    backs = []
    if kind == 0:
        backs = [pltpu.make_async_copy(wo, outs[4], own_sem.at[3])]
        for t in range(3):
            backs.append(pltpu.make_async_copy(w.at[t, :, TOFF:HALF], outs[5].at[t], own_sem.at[t]))
        for c in backs:
            c.start()
    allowed = mask_ref[kind] > 0
    sums = [[None] * 5 for _ in range(4)]
    for h in range(8):
        s = kind * 64 + HEAD_SIZE * h
        t0, t1 = s // 128, (s + HEAD_SIZE - 1) // 128 + 1
        win = slice(t0 * 128, t1 * 128)
        lane = lax.broadcasted_iota(jnp.int32, (1, (t1 - t0) * 128), 1) + t0 * 128
        ours = jnp.logical_and(lane >= s, lane < s + HEAD_SIZE).astype(F32).astype(BF)
        qh, kh, vh, uh = (a[:, win] * ours for a in (q, k, v, u))
        sc = jnp.where(allowed, nt(kh, qh) * factor, NEG)
        e = jnp.exp(sc - jnp.max(sc, 0, keepdims=True))
        p = e * (1.0 / jnp.sum(e, 0, keepdims=True))
        pb = p.astype(BF)
        gp = nt(vh, uh)
        pg = p * gp
        gs = ((pg - p * jnp.sum(pg, 0, keepdims=True)) * factor).astype(BF)
        res = (tn(gs, kh), nn(gs, qh), nn(pb, uh), tn(pb, vh))
        for j, r in enumerate(res):
            for t in range(t0, t1):
                part = r[:, (t - t0) * 128 : (t - t0 + 1) * 128]
                sums[j][t] = part if sums[j][t] is None else sums[j][t] + part
        for t in range(5):
            if s < (t + 1) * 128 <= s + HEAD_SIZE or (h == 7 and t == 4):
                for j in range(4):
                    g4[j // 2, j % 2, :, t * 128 : (t + 1) * 128] = sums[j][t].astype(BF)
    gone = [
        pltpu.make_async_copy(g4.at[core], keep_ref, own_sem.at[4]),
        pltpu.make_async_copy(g4.at[1 - core], send_ref, own_sem.at[5]),
    ]
    for c in gone:
        c.start()
    gh = nt(g4[0, 0], w[0]) + nt(g4[0, 1], w[1]) + nt(g4[1, 0], w[2])
    if kind == 0:
        outs[2][...] = g4[1, 1]
        outs[3][...] = gh
    else:
        outs[2][:, :HALF] = g4[1, 1]
        outs[2][:, HALF:] = gh.astype(BF)
    for c in backs + gone:
        c.wait()


def attend_call(kind, coord, mask, hid, cot, w_qkv, w_out, edge, pieces, plan):
    s = jax.ShapeDtypeStruct
    both = s((2, TOK, HALF), BF)
    if kind == 0:
        outs, specs = (s((TOK, HALF), BF), s((TOK, D), F32), s((D, D), BF), s((3, D, 128), BF)), (VM, VM, HBM, HBM)
    else:
        outs, specs = (s((TOK, HALF + D), BF), s((D, TOK), BF), s((D, TOK), BF)), (VM,) * 3
    return pl.pallas_call(
        lambda *refs: attend_kernel(kind, plan, len(pieces), *refs),
        out_shape=(both, both) + outs,
        in_specs=[SM] + [VM] * 3 + [HBM] * (3 + len(pieces)),
        out_specs=(HBM, HBM) + specs,
        scratch_shapes=[
            pltpu.VMEM((3, D, HALF), BF),
            pltpu.VMEM((D, D), BF),
            pltpu.VMEM((2, 2, TOK, HALF), BF),
            pltpu.SemaphoreType.DMA((len(plan), 2)),
            pltpu.SemaphoreType.DMA((7,)),
        ],
        compiler_params=PARAMS,
        cost_estimate=pl.CostEstimate(flops=(14, 6)[kind] * 10**9, bytes_accessed=16 * 10**6, transcendentals=10**6),
        name=("attend_space", "attend_time")[kind],
    )(coord, mask, hid, cot, w_qkv, w_out, edge, *pieces)


SHIP0 = ((0, (1, 2)), (0, (0, 3)), (1, (3, 2)), (1, (0, 1)))
SHIP1 = ((1, (0, 1)), (1, (2, 3)), (0, (0, 1, 2, 3)))


def weight_kernel(index, coord, hft, hpt, hft2, hpt2, cf, pos, cf2, pos2, kf, kp, rf, rp, *refs):
    outs, (held, sem) = refs[:-2], refs[-2:]
    core, zl, y = coord[0], coord[1], coord[2]

    def by_hidden(x, out):
        tiles = [((0, 256), None), ((256, 512), None), ((512, 640), (0, 128)), (None, (128, 384)), (None, (384, 640))]
        at = 0
        for f, p in tiles:
            parts = []
            if f is not None:
                sl = slice(*f)
                parts += [nn(hft[...], kf[x, :, sl]), nn(hft2[...], rf[x, :, sl])]
            if p is not None:
                sl = slice(*p)
                parts += [nn(hpt[...], kp[x, :, sl]), nn(hpt2[...], rp[x, :, sl])]
            total = sum(parts[1:], parts[0])
            out[:, at : at + total.shape[1]] = total.astype(BF)
            at += total.shape[1]

    def by_attended(x, out):
        for c in range(0, D, 384):
            sl = slice(c, c + 384)
            f = tn(kf[x], cf[:, sl]) + tn(rf[x], cf2[:, sl])
            ps = slice(D + c, D + c + 384)
            p = tn(kp[x], pos[:, ps]) + tn(rp[x], pos2[:, ps])
            out[0:512, sl] = f[:512].astype(BF)
            out[512:640, sl] = (f[512:] + p[:128]).astype(BF)
            out[640:1152, sl] = p[128:].astype(BF)

    if index == 0:
        by_hidden(0, held)
    else:

        @pl.when(core == 0)
        def _():
            by_hidden(1, held)

        @pl.when(core == 1)
        def _():
            by_attended(1, held)

    copies = []
    for r, ((a, order), out) in enumerate(zip((SHIP0, SHIP1)[index], outs)):
        for i, j in enumerate(order):
            rep = lax.rem(zl + a, 2) * 4 + jnp.bitwise_xor(y, j)
            rows = pl.ds(pl.multiple_of(rep * ROWS, 16), ROWS)
            c = pltpu.make_async_copy(held.at[rows, :], out.at[i], sem.at[r, i])
            c.start()
            copies.append(c)
    for c in copies:
        c.wait()


def weight_call(index, coord, *args):
    outs = tuple(jax.ShapeDtypeStruct((len(o), ROWS, D), BF) for _, o in (SHIP0, SHIP1)[index])
    cot = HBM if index == 0 else VM
    return pl.pallas_call(
        lambda *refs: weight_kernel(index, *refs),
        out_shape=outs,
        in_specs=[SM] + [VM] * 4 + [cot] * 4 + [VM] * 4,
        out_specs=(HBM,) * len(outs),
        scratch_shapes=[pltpu.VMEM((D, D), BF), pltpu.SemaphoreType.DMA((4, 4))],
        compiler_params=PARAMS,
        cost_estimate=pl.CostEstimate(flops=3 * 10**9, bytes_accessed=8 * 10**6, transcendentals=0),
        name="weight_grads",
    )(coord, *args)


def finish_kernel(lat_ref, cot_ref, att_ref, ghf_ref, back_ref, wo_ref, out_ref, gl_ref):
    lat = lat_ref[...]
    mixed = nn(att_ref[...], wo_ref[0:HALF, :]) + nn(back_ref[:, :HALF], wo_ref[TOFF:D, :])
    out_ref[...] = (lat.astype(F32) + mixed).astype(BF)
    normed, r = normalize(lat)
    gh = ghf_ref[...] + back_ref[:, HALF:].astype(F32)
    mean = jnp.mean(gh, -1, keepdims=True)
    dot = jnp.mean(gh * normed, -1, keepdims=True)
    gl_ref[...] = (cot_ref[...].astype(F32) + r * (gh - mean - normed * dot)).astype(BF)


def finish_call(*args):
    s = jax.ShapeDtypeStruct((TOK, D), BF)
    return pl.pallas_call(
        finish_kernel,
        out_shape=(s, s),
        in_specs=[VM] * 6,
        out_specs=(VM, VM),
        compiler_params=PARAMS,
        cost_estimate=pl.CostEstimate(flops=10**9, bytes_accessed=8 * 10**6, transcendentals=0),
        name="finish",
    )(*args)


def pairs(move):
    out = []
    for x in range(4):
        for z in range(8):
            for c in range(2):
                for y in range(4):
                    to = move(x, y, z, c)
                    spot = []
                    for xx, yy, zz, cc in ((x, y, z, c), (to[0] % 4, to[1] % 4, to[2] % 8, to[3])):
                        spot.append(((xx * 4 + zz // 2) * 2 + cc) * 8 + (zz % 2) * 4 + yy)
                    out.append(tuple(spot))
    return out


CORE = pairs(lambda x, y, z, c: (x, y, z, 1 - c))
XP = [pairs(lambda x, y, z, c, d=d: (x + d, y, z, c)) for d in range(4)]
YP = [pairs(lambda x, y, z, c, d=d: (x, y + d, z, c)) for d in range(4)]
ZP = [pairs(lambda x, y, z, c, d=d: (x, y, z + d, c)) for d in range(8)]
Y1 = pairs(lambda x, y, z, c: (x, y ^ 1, z, c))
Y3 = pairs(lambda x, y, z, c: (x, y ^ 3, z, c))
Z1 = pairs(lambda x, y, z, c: (x, y, z ^ 1, c))
Z1B = pairs(lambda x, y, z, c: (x, y, (z + 1 if z % 2 else z - 1), c))


def move(a, p):
    return lax.ppermute(a, AXES, p)


def add(*terms):
    total = terms[0].astype(F32)
    for t in terms[1:]:
        total = total + t.astype(F32)
    return total


def gather_weights(coord, w_qkv, w_out, early):
    e, g, z0, z1 = pack_call(coord, w_qkv, w_out)
    e_pieces, e_plan, g_pieces, g_plan = [], [], [], []

    def note(pieces, plan, array, parts):
        for other in (False, True):
            i = len(pieces)
            pieces.append(move(array, CORE) if other else array)
            for n, (name, dz, dy) in enumerate(parts):
                plan.append((lambda r, i=i, n=n: r[i].at[n], name, other, dz, dy))

    up, down = move(e, YP[1]), move(e, YP[3])
    z0, z1 = move(z0, ZP[1]), move(z1, ZP[7])
    z = jnp.stack([z0[:, :768], z1[:, :768]])
    gz = jnp.concatenate([z0[:, 768:], z1[:, 768:]], 1)
    zup, zdown = move(z, YP[1]), move(z, YP[3])
    up, down, *early = lax.optimization_barrier((up, down, *early))
    lat_cot, *early = early
    pos = lax.all_to_all(lat_cot, "tm", split_axis=0, concat_axis=0, tiled=True).reshape(TOK, 2 * D)
    relays = [move(up[0], YP[1]), move(down[1], YP[3]), move(zup[0], YP[1]), move(zdown[1], YP[3])]
    *relays, g, gz = lax.optimization_barrier((*relays, g, gz))
    gg = jnp.stack([g, gz])
    g_all = (gz[None], move(gg, YP[1]), move(gg, YP[3]), move(gg, YP[2]))
    for array, dz, dy in ((z, 1, 0), (up, 0, 3), (down, 0, 1), (zup, 1, 3), (zdown, 1, 1)):
        note(e_pieces, e_plan, array, (("e0", dz, dy), ("e1", dz, dy)))
    for n, array in enumerate(relays):
        note(e_pieces, e_plan, array[None], ((("e0", "e1")[n % 2], n // 2, 2),))

    def second(after, pos):
        after, pos, *arrays = lax.optimization_barrier((after, pos, *g_all))
        note(g_pieces, g_plan, arrays[0], (("g", 1, 0),))
        for array, dy in zip(arrays[1:], (3, 1, 2)):
            note(g_pieces, g_plan, array, (("g", 0, dy), ("g", 1, dy)))
        return after, pos, g_pieces, g_plan

    return (e_pieces, e_plan), second, pos, early


def all_sum(own):
    x = lax.axis_index("tm") // 8
    parts = own.reshape(4, 72, D)

    def part(i):
        return lax.dynamic_index_in_dim(parts, i % 4, 0, keepdims=False)

    got = [move(part(x + d), XP[d]) for d in (1, 2, 3)]
    mine = add(part(x), *got).astype(BF)
    two, four, six = (move(mine, ZP[d]) for d in (2, 4, 6))
    row = (add(mine, four) + add(two, six)).astype(BF)
    ring = jnp.stack([row] + [move(row, XP[d]) for d in (1, 2, 3)])
    return jnp.take(ring, (x - jnp.arange(4)) % 4, axis=0).reshape(2, ROWS, D)


def reduce_out0(s0a, k0a, s0b, k0b):
    ga, gb = move(s0a, Y1), move(s0b, Y3)
    ka, kb = add(k0a, ga).astype(BF), add(k0b, gb).astype(BF)
    ga, gb = move(ka[1], Y3), move(kb[1], Y1)
    ours, theirs = add(ka[0], ga), add(kb[0], gb).astype(BF)
    return add(ours, move(theirs, Z1)).astype(BF)


def reduce_out1(sa, sb, keep):
    ga, gb = move(sa, Z1), move(sb, Z1B)
    b = [add(keep[0], ga[0]), add(keep[1], ga[1]), add(keep[2], gb[0]), add(keep[3], gb[1])]
    b = [t.astype(BF) for t in b]
    top, low = [t[:72] for t in b], [t[72:] for t in b]
    gt = move(jnp.stack([top[1], top[2]]), Y1)
    gl = move(jnp.stack([low[3], low[2]]), Y3)
    t0, t3 = add(top[0], gt[0]).astype(BF), add(top[3], gt[1]).astype(BF)
    l0, l1 = add(low[0], gl[0]).astype(BF), add(low[1], gl[1]).astype(BF)
    gt, gl = move(t3, Y3), move(l1, Y1)
    return jnp.concatenate([add(t0, gt), add(l0, gl)]).astype(BF)


def local(latents, cotangent, w_qkv, w_out, tile_pattern):
    tm, rep = lax.axis_index("tm"), lax.axis_index("replica")
    core, zl, y = tm % 2, rep // 4, rep % 4
    coord = jnp.stack([core, zl, y]).astype(jnp.int32)
    lat, cot = latents.reshape(TOK, D), cotangent.reshape(TOK, D)
    lat_cot = jnp.concatenate([lat, cot], 1).reshape(32, 8, 2 * D)
    early = (lat_cot, *norm_call(tile_pattern, lat), move(cot, CORE))
    e_part, second, pos, early = gather_weights(coord, w_qkv, w_out, early)
    hf, hft, mask, cf2 = early

    kf, sf, att, ghf, wo, edge = attend_call(0, coord, mask, hf, cot, w_qkv, w_out, w_out, *e_part)
    edge, pos, *g_part = second(edge, pos)
    pos2 = move(pos, CORE)
    rf, hft2 = move(sf, CORE), move(hft, CORE)
    kp, sp, back, hpt, hpt2 = attend_call(1, coord, mask, pos, pos2, w_qkv, wo, edge, *g_part)
    sp, rf, hft2 = lax.optimization_barrier((sp, rf, hft2))
    rp = move(sp, CORE)
    terms = (coord, hft, hpt, hft2, hpt2, cot, pos, cf2, pos2, kf, kp, rf, rp)
    w0, w1 = weight_call(0, *terms), weight_call(1, *terms)
    *w1, back = lax.optimization_barrier((*w1, back))
    back = lax.all_to_all(
        back.reshape(32, 8, HALF + D), "tm", split_axis=0, concat_axis=0, tiled=True
    ).reshape(TOK, HALF + D)
    own = jnp.concatenate([reduce_out0(*w0), reduce_out1(*w1)])
    own, back = lax.optimization_barrier((own, back))
    result, grad_input = finish_call(lat, cot, att, ghf, back, wo)
    total = all_sum(own)
    other = move(total, CORE)
    factor = 1.0 / math.sqrt(65536)
    first = core == 0
    q, k = (jnp.where(first, total[i], other[i]) for i in range(2))
    v, o = (jnp.where(first, other[i], total[i]) for i in range(2))
    dw_qkv = jnp.concatenate([q, k, v], 1).astype(F32) * factor
    dw_out = o.astype(F32) * factor
    return result.reshape(1, 1, TOK, D), grad_input.reshape(1, 1, TOK, D), dw_qkv, dw_out


def solution(mesh):
    tokens, rows = P("replica", "tm", None, None), P("replica", None)
    return jax.shard_map(
        local,
        mesh=mesh,
        in_specs=(tokens, tokens, rows, rows, P()),
        out_specs=(tokens, tokens, rows, rows),
        check_vma=False,
    )
```

```python
import math

import jax
import jax.numpy as jnp
from jax import lax
from jax.experimental import pallas as pl
from jax.experimental.pallas import tpu as pltpu
from jax.sharding import PartitionSpec as P

HEADS = 16
HEAD_SIZE = 72
SPATIAL_HEADS = 8
TOK = 256
D = 1152
HALF = 640
TOFF = 512
ROWS = 144
BF = jnp.bfloat16
F32 = jnp.float32
NEG = -1e30
VMEM_LIMIT = 60 * 1024 * 1024
AXES = ("tm", "replica")
HBM = pl.BlockSpec(memory_space=pl.ANY)
VM = pl.BlockSpec(memory_space=pltpu.VMEM)
SM = pl.BlockSpec(memory_space=pltpu.SMEM)
PARAMS = pltpu.CompilerParams(vmem_limit_bytes=VMEM_LIMIT)


def nn(a, b):
    return lax.dot_general(a, b, (((1,), (0,)), ((), ())), preferred_element_type=F32)


def nt(a, b):
    return lax.dot_general(a, b, (((1,), (1,)), ((), ())), preferred_element_type=F32)


def tn(a, b):
    return lax.dot_general(a, b, (((0,), (0,)), ((), ())), preferred_element_type=F32)


def normalize(x):
    x = x.astype(F32)
    centred = x - jnp.mean(x, -1, keepdims=True)
    r = lax.rsqrt(jnp.mean(centred * centred, -1, keepdims=True) + 1e-06)
    return centred * r, r


def pack_kernel(coord, wqkv_ref, wout_ref, e_ref, g_ref, z0_ref, z1_ref):
    q, k, v = 0, D, 2 * D

    @pl.when(coord[0] == 0)
    def _():
        e_ref[0, :, 0:640] = wqkv_ref[:, q : q + 640]
        e_ref[0, :, 640:768] = wqkv_ref[:, k : k + 128]
        e_ref[1, :, 0:512] = wqkv_ref[:, k + 128 : k + 640]
        e_ref[1, :, 512:768] = wqkv_ref[:, v : v + 256]
        g_ref[:, 0:512] = wqkv_ref[:, q + 640 : q + D]
        g_ref[:, 512:768] = wqkv_ref[:, v + 640 : v + 896]

    @pl.when(coord[0] == 1)
    def _():
        e_ref[0, :, 0:384] = wqkv_ref[:, v + 256 : v + 640]
        e_ref[0, :, 384:768] = wout_ref[:, 0:384]
        e_ref[1, :, :] = wout_ref[:, 384:]
        g_ref[:, 0:512] = wqkv_ref[:, k + 640 : k + D]
        g_ref[:, 512:768] = wqkv_ref[:, v + 896 : v + D]

    for n, z_ref in enumerate((z0_ref, z1_ref)):
        z_ref[:, 0:768] = e_ref[n]
        z_ref[:, 768:] = g_ref[:, 384 * n : 384 * (n + 1)]


def pack_call(coord, w_qkv, w_out):
    s = jax.ShapeDtypeStruct
    return pl.pallas_call(
        pack_kernel,
        out_shape=(s((2, ROWS, 768), BF), s((ROWS, 768), BF)) + (s((ROWS, D), BF),) * 2,
        in_specs=[SM, VM, VM],
        out_specs=(VM,) * 4,
        compiler_params=PARAMS,
        cost_estimate=pl.CostEstimate(flops=0, bytes_accessed=2 * 10**6, transcendentals=0),
        name="pack",
    )(coord, w_qkv, w_out)


def norm_kernel(tile_ref, src_ref, h_ref, ht_ref, mask_ref):
    n, _ = normalize(src_ref[...])
    h_ref[...] = n.astype(BF)
    ht_ref[...] = n.T.astype(BF)
    row = lax.broadcasted_iota(jnp.int32, (TOK, TOK), 0)
    col = lax.broadcasted_iota(jnp.int32, (TOK, TOK), 1)
    mask_ref[1] = (row % 8 == col % 8).astype(F32)
    col = lax.broadcasted_iota(jnp.int32, (64, TOK), 1) // 64
    for i in range(4):
        line = jnp.zeros((64, TOK), F32)
        for j in range(4):
            line = jnp.where(col == j, (tile_ref[j, i] == 1).astype(F32), line)
        mask_ref[0, 64 * i : 64 * (i + 1), :] = line


def norm_call(tile_pattern, src):
    s = jax.ShapeDtypeStruct
    outs = (s((TOK, D), BF), s((D, TOK), BF), s((2, TOK, TOK), F32))
    return pl.pallas_call(
        norm_kernel,
        out_shape=outs,
        in_specs=[SM, VM],
        out_specs=(VM,) * len(outs),
        compiler_params=PARAMS,
        cost_estimate=pl.CostEstimate(flops=10**8, bytes_accessed=2 * 10**6, transcendentals=0),
        name="norm",
    )(tile_pattern, src)


SPREAD = {
    "e0": (((0, 640, 0, 0), (640, 768, 1, 0)), ((0, 384, 2, 256), (384, 768, 3, 0))),
    "e1": (((0, 512, 1, 128), (512, 768, 2, 0)), ((0, 768, 3, 384),)),
    "g": (((0, 512, 0, 128), (512, 768, 2, 128)), ((0, 512, 1, 128), (512, 768, 2, 384))),
}


def load_weights(plan, pieces, w, wo, sem, coord):
    core, zl, y = coord[0], coord[1], coord[2]
    waits = []
    for n, (view, name, other, dz, dy) in enumerate(plan):
        rep = lax.rem(zl + dz, 2) * 4 + lax.rem(y + dy, 4)
        rows = pl.ds(pl.multiple_of(rep * ROWS, 16), ROWS)
        src = view(pieces)
        owner = 1 - core if other else core
        for c, spread in enumerate(SPREAD[name]):
            copies = []
            for k, (c0, c1, quarter, to) in enumerate(spread):
                dst = wo.at[rows, to : to + c1 - c0] if quarter == 3 else w.at[quarter, rows, to : to + c1 - c0]
                copies.append(pltpu.make_async_copy(src.at[:, c0:c1], dst, sem.at[n, k]))

            @pl.when(owner == c)
            def _(copies=copies):
                for d in copies:
                    d.start()

            waits.append((owner == c, copies))

    def wait():
        for when, copies in waits:

            @pl.when(when)
            def _(copies=copies):
                for d in copies:
                    d.wait()

    return wait


def attend_kernel(kind, plan, n_piece, *refs):
    coord, mask_ref, hid_ref, cot_ref, wqkv_ref, wout_ref, edge_ref = refs[:7]
    pieces = refs[7 : 7 + n_piece]
    outs = refs[7 + n_piece : -5]
    w, wo, g4, sem, own_sem = refs[-5:]
    keep_ref, send_ref = outs[:2]
    core, zl, y = coord[0], coord[1], coord[2]
    cols = slice(kind * TOFF, kind * TOFF + HALF)
    wait = load_weights(plan, pieces, w, wo, sem, coord)
    rows = pl.ds(pl.multiple_of((zl * 4 + y) * ROWS, 16), ROWS)
    copies = []
    for t in range(3):
        if kind == 0:
            src, dst = wqkv_ref.at[:, t * D : t * D + HALF], w.at[t, rows, :]
        else:
            src, dst = wqkv_ref.at[:, t * D + HALF : (t + 1) * D], w.at[t, rows, 128:]
            copies.append(pltpu.make_async_copy(edge_ref.at[t], w.at[t, :, 0:128], own_sem.at[4 + t]))
        copies.append(pltpu.make_async_copy(src, dst, own_sem.at[t]))
    if kind == 0:
        copies.append(pltpu.make_async_copy(wout_ref, wo.at[rows, :], own_sem.at[3]))
    else:
        copies.append(pltpu.make_async_copy(wout_ref, wo, own_sem.at[3]))
    for c in copies:
        c.start()
    if kind == 1:
        normed, _ = normalize(hid_ref[:, :D])
        hid = normed.astype(BF)
        cot = hid_ref[:, D:]
        outs[3][...] = normed.T.astype(BF)
        outs[4][...] = cot
    else:
        hid, cot = hid_ref[...], cot_ref[...]
    for c in copies:
        c.wait()
    wait()
    if kind == 0:
        backs = [pltpu.make_async_copy(wo, outs[4], own_sem.at[3])]
        for t in range(3):
            backs.append(pltpu.make_async_copy(w.at[t, :, TOFF:HALF], outs[5].at[t], own_sem.at[t]))
        for c in backs:
            c.start()
    factor = 1.0 / math.sqrt(HEAD_SIZE)
    q = nn(hid, w[0]).astype(BF)
    k = nn(hid, w[1]).astype(BF)
    v = nn(hid, w[2]).astype(BF)
    u = nt(cot, wo[cols, :]).astype(BF)
    allowed = mask_ref[kind] > 0
    sums = [[None] * 5 for _ in range(4)]
    for h in range(8):
        s = kind * 64 + HEAD_SIZE * h
        t0, t1 = s // 128, (s + HEAD_SIZE - 1) // 128 + 1
        win = slice(t0 * 128, t1 * 128)
        lane = lax.broadcasted_iota(jnp.int32, (1, (t1 - t0) * 128), 1) + t0 * 128
        ours = jnp.logical_and(lane >= s, lane < s + HEAD_SIZE).astype(F32).astype(BF)
        qh, kh, vh, uh = (a[:, win] * ours for a in (q, k, v, u))
        sc = jnp.where(allowed, nt(kh, qh) * factor, NEG)
        e = jnp.exp(sc - jnp.max(sc, 0, keepdims=True))
        p = e * (1.0 / jnp.sum(e, 0, keepdims=True))
        pb = p.astype(BF)
        gp = nt(vh, uh)
        pg = p * gp
        gs = ((pg - p * jnp.sum(pg, 0, keepdims=True)) * factor).astype(BF)
        res = (tn(gs, kh), nn(gs, qh), nn(pb, uh), tn(pb, vh))
        for j, r in enumerate(res):
            for t in range(t0, t1):
                part = r[:, (t - t0) * 128 : (t - t0 + 1) * 128]
                sums[j][t] = part if sums[j][t] is None else sums[j][t] + part
        for t in range(5):
            if s < (t + 1) * 128 <= s + HEAD_SIZE or (h == 7 and t == 4):
                for j in range(4):
                    g4[j // 2, j % 2, :, t * 128 : (t + 1) * 128] = sums[j][t].astype(BF)
    gh = nt(g4[0, 0], w[0]) + nt(g4[0, 1], w[1]) + nt(g4[1, 0], w[2])
    if kind == 0:
        outs[2][...] = g4[1, 1]
        outs[3][...] = gh
    else:
        outs[2][:, :HALF] = g4[1, 1]
        outs[2][:, HALF:] = gh.astype(BF)
    keep_ref[...] = g4[core]
    send_ref[...] = g4[1 - core]
    if kind == 0:
        for c in backs:
            c.wait()


def attend_call(kind, coord, mask, hid, cot, w_qkv, w_out, edge, pieces, plan):
    s = jax.ShapeDtypeStruct
    both = s((2, TOK, HALF), BF)
    if kind == 0:
        outs, specs = (s((TOK, HALF), BF), s((TOK, D), F32), s((D, D), BF), s((3, D, 128), BF)), (VM, VM, HBM, HBM)
    else:
        outs, specs = (s((TOK, HALF + D), BF), s((D, TOK), BF), s((TOK, D), BF)), (VM,) * 3
    return pl.pallas_call(
        lambda *refs: attend_kernel(kind, plan, len(pieces), *refs),
        out_shape=(both, both) + outs,
        in_specs=[SM] + [VM] * 3 + [HBM] * (3 + len(pieces)),
        out_specs=(VM, VM) + specs,
        scratch_shapes=[
            pltpu.VMEM((3, D, HALF), BF),
            pltpu.VMEM((D, D), BF),
            pltpu.VMEM((2, 2, TOK, HALF), BF),
            pltpu.SemaphoreType.DMA((len(plan), 2)),
            pltpu.SemaphoreType.DMA((7,)),
        ],
        compiler_params=PARAMS,
        cost_estimate=pl.CostEstimate(flops=6 * 10**9, bytes_accessed=16 * 10**6, transcendentals=10**6),
        name=("attend_space", "attend_time")[kind],
    )(coord, mask, hid, cot, w_qkv, w_out, edge, *pieces)


SHIP0 = ((0, (1, 2)), (0, (0, 3)), (1, (3, 2)), (1, (0, 1)))
SHIP1 = ((1, (0, 1)), (1, (2, 3)), (0, (0, 1, 2, 3)))


def weight_kernel(coord, hft, hpt, hft2, hpt2, cf, cp, cf2, cp2, kf, kp, rf, rp, *refs):
    outs, (a0, a1, sem) = refs[:7], refs[7:]
    core, zl, y = coord[0], coord[1], coord[2]

    def by_hidden(x, out):
        tiles = [((0, 256), None), ((256, 512), None), ((512, 640), (0, 128)), (None, (128, 384)), (None, (384, 640))]
        at = 0
        for f, p in tiles:
            parts = []
            if f is not None:
                sl = slice(*f)
                parts += [nn(hft[...], kf[x, :, sl]), nn(hft2[...], rf[x, :, sl])]
            if p is not None:
                sl = slice(*p)
                parts += [nn(hpt[...], kp[x, :, sl]), nn(hpt2[...], rp[x, :, sl])]
            total = sum(parts[1:], parts[0])
            out[:, at : at + total.shape[1]] = total.astype(BF)
            at += total.shape[1]

    def by_attended(x, out):
        for c in range(0, D, 384):
            sl = slice(c, c + 384)
            f = tn(kf[x], cf[:, sl]) + tn(rf[x], cf2[:, sl])
            p = tn(kp[x], cp[:, sl]) + tn(rp[x], cp2[:, sl])
            out[0:512, sl] = f[:512].astype(BF)
            out[512:640, sl] = (f[512:] + p[:128]).astype(BF)
            out[640:1152, sl] = p[128:].astype(BF)

    def ship(scratch, ships, refs, n):
        copies = []
        for r, ((a, order), out) in enumerate(zip(ships, refs)):
            for i, j in enumerate(order):
                rep = lax.rem(zl + a, 2) * 4 + jnp.bitwise_xor(y, j)
                rows = pl.ds(pl.multiple_of(rep * ROWS, 16), ROWS)
                c = pltpu.make_async_copy(scratch.at[rows, :], out.at[i], sem.at[n, r, i])
                c.start()
                copies.append(c)
        return copies

    by_hidden(0, a0)
    c0 = ship(a0, SHIP0, outs[:4], 0)

    @pl.when(core == 0)
    def _():
        by_hidden(1, a1)

    @pl.when(core == 1)
    def _():
        by_attended(1, a1)

    c1 = ship(a1, SHIP1, outs[4:], 1)
    for c in c0 + c1:
        c.wait()


def weight_call(coord, *args):
    outs = tuple(jax.ShapeDtypeStruct((len(o), ROWS, D), BF) for _, o in SHIP0 + SHIP1)
    return pl.pallas_call(
        weight_kernel,
        out_shape=outs,
        in_specs=[SM] + [VM] * len(args),
        out_specs=(HBM,) * len(outs),
        scratch_shapes=[pltpu.VMEM((D, D), BF), pltpu.VMEM((D, D), BF), pltpu.SemaphoreType.DMA((2, 4, 4))],
        compiler_params=PARAMS,
        cost_estimate=pl.CostEstimate(flops=6 * 10**9, bytes_accessed=16 * 10**6, transcendentals=0),
        name="weight_grads",
    )(coord, *args)


def finish_kernel(lat_ref, cot_ref, att_ref, ghf_ref, back_ref, wo_ref, out_ref, gl_ref):
    lat = lat_ref[...]
    mixed = nn(att_ref[...], wo_ref[0:HALF, :]) + nn(back_ref[:, :HALF], wo_ref[TOFF:D, :])
    out_ref[...] = (lat.astype(F32) + mixed).astype(BF)
    normed, r = normalize(lat)
    gh = ghf_ref[...] + back_ref[:, HALF:].astype(F32)
    mean = jnp.mean(gh, -1, keepdims=True)
    dot = jnp.mean(gh * normed, -1, keepdims=True)
    gl_ref[...] = (cot_ref[...].astype(F32) + r * (gh - mean - normed * dot)).astype(BF)


def finish_call(*args):
    s = jax.ShapeDtypeStruct((TOK, D), BF)
    return pl.pallas_call(
        finish_kernel,
        out_shape=(s, s),
        in_specs=[VM] * 6,
        out_specs=(VM, VM),
        compiler_params=PARAMS,
        cost_estimate=pl.CostEstimate(flops=10**9, bytes_accessed=8 * 10**6, transcendentals=0),
        name="finish",
    )(*args)


def pairs(move):
    out = []
    for x in range(4):
        for z in range(8):
            for c in range(2):
                for y in range(4):
                    to = move(x, y, z, c)
                    spot = []
                    for xx, yy, zz, cc in ((x, y, z, c), (to[0] % 4, to[1] % 4, to[2] % 8, to[3])):
                        spot.append(((xx * 4 + zz // 2) * 2 + cc) * 8 + (zz % 2) * 4 + yy)
                    out.append(tuple(spot))
    return out


CORE = pairs(lambda x, y, z, c: (x, y, z, 1 - c))
XP = [pairs(lambda x, y, z, c, d=d: (x + d, y, z, c)) for d in range(4)]
YP = [pairs(lambda x, y, z, c, d=d: (x, y + d, z, c)) for d in range(4)]
ZP = [pairs(lambda x, y, z, c, d=d: (x, y, z + d, c)) for d in range(8)]
Y1 = pairs(lambda x, y, z, c: (x, y ^ 1, z, c))
Y3 = pairs(lambda x, y, z, c: (x, y ^ 3, z, c))
Z1 = pairs(lambda x, y, z, c: (x, y, z ^ 1, c))
Z1B = pairs(lambda x, y, z, c: (x, y, (z + 1 if z % 2 else z - 1), c))


def move(a, p):
    return lax.ppermute(a, AXES, p)


def add(*terms):
    total = terms[0].astype(F32)
    for t in terms[1:]:
        total = total + t.astype(F32)
    return total


def gather_weights(coord, w_qkv, w_out, early):
    e, g, z0, z1 = pack_call(coord, w_qkv, w_out)
    e_pieces, e_plan, g_pieces, g_plan = [], [], [], []

    def note(pieces, plan, array, parts):
        for other in (False, True):
            i = len(pieces)
            pieces.append(move(array, CORE) if other else array)
            for n, (name, dz, dy) in enumerate(parts):
                plan.append((lambda r, i=i, n=n: r[i].at[n], name, other, dz, dy))

    up, down = move(e, YP[1]), move(e, YP[3])
    z0, z1 = move(z0, ZP[1]), move(z1, ZP[7])
    z = jnp.stack([z0[:, :768], z1[:, :768]])
    gz = jnp.concatenate([z0[:, 768:], z1[:, 768:]], 1)
    zup, zdown = move(z, YP[1]), move(z, YP[3])
    up, down, *early = lax.optimization_barrier((up, down, *early))
    lat_cot, *early = early
    pos = lax.all_to_all(lat_cot, "tm", split_axis=0, concat_axis=0, tiled=True).reshape(TOK, 2 * D)
    relays = [move(up[0], YP[1]), move(down[1], YP[3]), move(zup[0], YP[1]), move(zdown[1], YP[3])]
    *relays, g, gz = lax.optimization_barrier((*relays, g, gz))
    gg = jnp.stack([g, gz])
    g_all = (gz[None], move(gg, YP[1]), move(gg, YP[3]), move(gg, YP[2]))
    for array, dz, dy in ((z, 1, 0), (up, 0, 3), (down, 0, 1), (zup, 1, 3), (zdown, 1, 1)):
        note(e_pieces, e_plan, array, (("e0", dz, dy), ("e1", dz, dy)))
    for n, array in enumerate(relays):
        note(e_pieces, e_plan, array[None], ((("e0", "e1")[n % 2], n // 2, 2),))

    def second(after):
        after, *arrays = lax.optimization_barrier((after, *g_all))
        note(g_pieces, g_plan, arrays[0], (("g", 1, 0),))
        for array, dy in zip(arrays[1:], (3, 1, 2)):
            note(g_pieces, g_plan, array, (("g", 0, dy), ("g", 1, dy)))
        return after, g_pieces, g_plan

    return (e_pieces, e_plan), second, pos, early


def all_sum(own):
    x = lax.axis_index("tm") // 8
    parts = own.reshape(4, 72, D)

    def part(i):
        return lax.dynamic_index_in_dim(parts, i % 4, 0, keepdims=False)

    got = [move(part(x + d), XP[d]) for d in (1, 2, 3)]
    mine = add(part(x), *got).astype(BF)
    two, four, six = (move(mine, ZP[d]) for d in (2, 4, 6))
    row = (add(mine, four) + add(two, six)).astype(BF)
    ring = jnp.stack([row] + [move(row, XP[d]) for d in (1, 2, 3)])
    return jnp.take(ring, (x - jnp.arange(4)) % 4, axis=0).reshape(2, ROWS, D)


def reduce_out0(k0a, k0b, ga, gb):
    ka, kb = add(k0a, ga).astype(BF), add(k0b, gb).astype(BF)
    ga, gb = move(ka[1], Y3), move(kb[1], Y1)
    ours, theirs = add(ka[0], ga), add(kb[0], gb).astype(BF)
    return add(ours, move(theirs, Z1)).astype(BF)


def reduce_out1(keep, ga, gb):
    b = [add(keep[0], ga[0]), add(keep[1], ga[1]), add(keep[2], gb[0]), add(keep[3], gb[1])]
    b = [t.astype(BF) for t in b]
    top, low = [t[:72] for t in b], [t[72:] for t in b]
    gt = move(jnp.stack([top[1], top[2]]), Y1)
    gl = move(jnp.stack([low[3], low[2]]), Y3)
    t0, t3 = add(top[0], gt[0]).astype(BF), add(top[3], gt[1]).astype(BF)
    l0, l1 = add(low[0], gl[0]).astype(BF), add(low[1], gl[1]).astype(BF)
    gt, gl = move(t3, Y3), move(l1, Y1)
    return jnp.concatenate([add(t0, gt), add(l0, gl)]).astype(BF)


def local(latents, cotangent, w_qkv, w_out, tile_pattern):
    tm, rep = lax.axis_index("tm"), lax.axis_index("replica")
    core, zl, y = tm % 2, rep // 4, rep % 4
    coord = jnp.stack([core, zl, y]).astype(jnp.int32)
    lat, cot = latents.reshape(TOK, D), cotangent.reshape(TOK, D)
    lat_cot = jnp.concatenate([lat, cot], 1).reshape(32, 8, 2 * D)
    early = (lat_cot, *norm_call(tile_pattern, lat), move(cot, CORE))
    e_part, second, pos, early = gather_weights(coord, w_qkv, w_out, early)
    hf, hft, mask, cf2 = early

    kf, sf, att, ghf, wo, edge = attend_call(0, coord, mask, hf, cot, w_qkv, w_out, w_out, *e_part)
    edge, *g_part = second(edge)
    rf, hft2 = move(sf, CORE), move(hft, CORE)
    kp, sp, back, hpt, cp = attend_call(1, coord, mask, pos, cot, w_qkv, wo, edge, *g_part)
    sp, rf, hft2 = lax.optimization_barrier((sp, rf, hft2))
    rp, hpt2, cp2 = move(sp, CORE), move(hpt, CORE), move(cp, CORE)
    terms = (coord, hft, hpt, hft2, hpt2, cot, cp, cf2, cp2, kf, kp, rf, rp)
    back = lax.all_to_all(
        back.reshape(32, 8, HALF + D), "tm", split_axis=0, concat_axis=0, tiled=True
    ).reshape(TOK, HALF + D)
    w = weight_call(*terms)
    first = (move(w[0], Y1), move(w[2], Y3), move(w[4], Z1), move(w[5], Z1B))
    *first, back = lax.optimization_barrier((*first, back))
    own = jnp.concatenate([reduce_out0(w[1], w[3], *first[:2]), reduce_out1(w[6], *first[2:])])
    result, grad_input = finish_call(lat, cot, att, ghf, back, wo)
    total = all_sum(own)
    other = move(total, CORE)
    factor = 1.0 / math.sqrt(65536)
    first = core == 0
    q, k = (jnp.where(first, total[i], other[i]) for i in range(2))
    v, o = (jnp.where(first, other[i], total[i]) for i in range(2))
    dw_qkv = jnp.concatenate([q, k, v], 1).astype(F32) * factor
    dw_out = o.astype(F32) * factor
    return result.reshape(1, 1, TOK, D), grad_input.reshape(1, 1, TOK, D), dw_qkv, dw_out


def solution(mesh):
    tokens, rows = P("replica", "tm", None, None), P("replica", None)
    return jax.shard_map(
        local,
        mesh=mesh,
        in_specs=(tokens, tokens, rows, rows, P()),
        out_specs=(tokens, tokens, rows, rows),
        check_vma=False,
    )
```

```python
import math

import jax
import jax.numpy as jnp
from jax import lax
from jax.experimental import pallas as pl
from jax.experimental.pallas import tpu as pltpu
from jax.sharding import PartitionSpec as P

HEADS = 16
HEAD_SIZE = 72
SPATIAL_HEADS = 8
TOK = 256
D = 1152
HALF = 640
TOFF = 512
ROWS = 144
BF = jnp.bfloat16
F32 = jnp.float32
NEG = -1e30
VMEM_LIMIT = 60 * 1024 * 1024
AXES = ("tm", "replica")
HBM = pl.BlockSpec(memory_space=pl.ANY)
VM = pl.BlockSpec(memory_space=pltpu.VMEM)
SM = pl.BlockSpec(memory_space=pltpu.SMEM)
PARAMS = pltpu.CompilerParams(vmem_limit_bytes=VMEM_LIMIT)


def nn(a, b):
    return lax.dot_general(a, b, (((1,), (0,)), ((), ())), preferred_element_type=F32)


def nt(a, b):
    return lax.dot_general(a, b, (((1,), (1,)), ((), ())), preferred_element_type=F32)


def tn(a, b):
    return lax.dot_general(a, b, (((0,), (0,)), ((), ())), preferred_element_type=F32)


def normalize(x):
    x = x.astype(F32)
    centred = x - jnp.mean(x, -1, keepdims=True)
    r = lax.rsqrt(jnp.mean(centred * centred, -1, keepdims=True) + 1e-06)
    return centred * r, r


def pack_kernel(coord, wqkv_ref, wout_ref, e_ref, g_ref, z0_ref, z1_ref):
    q, k, v = 0, D, 2 * D

    @pl.when(coord[0] == 0)
    def _():
        e_ref[0, :, 0:640] = wqkv_ref[:, q : q + 640]
        e_ref[0, :, 640:768] = wqkv_ref[:, k : k + 128]
        e_ref[1, :, 0:512] = wqkv_ref[:, k + 128 : k + 640]
        e_ref[1, :, 512:768] = wqkv_ref[:, v : v + 256]
        g_ref[:, 0:512] = wqkv_ref[:, q + 640 : q + D]
        g_ref[:, 512:768] = wqkv_ref[:, v + 640 : v + 896]

    @pl.when(coord[0] == 1)
    def _():
        e_ref[0, :, 0:384] = wqkv_ref[:, v + 256 : v + 640]
        e_ref[0, :, 384:768] = wout_ref[:, 0:384]
        e_ref[1, :, :] = wout_ref[:, 384:]
        g_ref[:, 0:512] = wqkv_ref[:, k + 640 : k + D]
        g_ref[:, 512:768] = wqkv_ref[:, v + 896 : v + D]

    for n, z_ref in enumerate((z0_ref, z1_ref)):
        z_ref[:, 0:768] = e_ref[n]
        z_ref[:, 768:] = g_ref[:, 384 * n : 384 * (n + 1)]


def pack_call(coord, w_qkv, w_out):
    s = jax.ShapeDtypeStruct
    return pl.pallas_call(
        pack_kernel,
        out_shape=(s((2, ROWS, 768), BF), s((ROWS, 768), BF)) + (s((ROWS, D), BF),) * 2,
        in_specs=[SM, VM, VM],
        out_specs=(VM,) * 4,
        compiler_params=PARAMS,
        cost_estimate=pl.CostEstimate(flops=0, bytes_accessed=2 * 10**6, transcendentals=0),
        name="pack",
    )(coord, w_qkv, w_out)


def norm_kernel(tile_ref, src_ref, h_ref, ht_ref, mask_ref):
    n, _ = normalize(src_ref[...])
    h_ref[...] = n.astype(BF)
    ht_ref[...] = n.T.astype(BF)
    row = lax.broadcasted_iota(jnp.int32, (TOK, TOK), 0)
    col = lax.broadcasted_iota(jnp.int32, (TOK, TOK), 1)
    mask_ref[1] = (row % 8 == col % 8).astype(F32)
    col = lax.broadcasted_iota(jnp.int32, (64, TOK), 1) // 64
    for i in range(4):
        line = jnp.zeros((64, TOK), F32)
        for j in range(4):
            line = jnp.where(col == j, (tile_ref[j, i] == 1).astype(F32), line)
        mask_ref[0, 64 * i : 64 * (i + 1), :] = line


def norm_call(tile_pattern, src):
    s = jax.ShapeDtypeStruct
    outs = (s((TOK, D), BF), s((D, TOK), BF), s((2, TOK, TOK), F32))
    return pl.pallas_call(
        norm_kernel,
        out_shape=outs,
        in_specs=[SM, VM],
        out_specs=(VM,) * len(outs),
        compiler_params=PARAMS,
        cost_estimate=pl.CostEstimate(flops=10**8, bytes_accessed=2 * 10**6, transcendentals=0),
        name="norm",
    )(tile_pattern, src)


SPREAD = {
    "e0": (((0, 640, 0, 0), (640, 768, 1, 0)), ((0, 384, 2, 256), (384, 768, 3, 0))),
    "e1": (((0, 512, 1, 128), (512, 768, 2, 0)), ((0, 768, 3, 384),)),
    "g": (((0, 512, 0, 128), (512, 768, 2, 128)), ((0, 512, 1, 128), (512, 768, 2, 384))),
}


def load_weights(plan, pieces, w, wo, sem, coord):
    core, zl, y = coord[0], coord[1], coord[2]
    waits = []
    for n, (view, name, other, dz, dy) in enumerate(plan):
        rep = lax.rem(zl + dz, 2) * 4 + lax.rem(y + dy, 4)
        rows = pl.ds(pl.multiple_of(rep * ROWS, 16), ROWS)
        src = view(pieces)
        owner = 1 - core if other else core
        for c, spread in enumerate(SPREAD[name]):
            copies = []
            for k, (c0, c1, quarter, to) in enumerate(spread):
                dst = wo.at[rows, to : to + c1 - c0] if quarter == 3 else w.at[quarter, rows, to : to + c1 - c0]
                copies.append(pltpu.make_async_copy(src.at[:, c0:c1], dst, sem.at[n, k]))

            @pl.when(owner == c)
            def _(copies=copies):
                for d in copies:
                    d.start()

            waits.append((owner == c, copies))

    def wait():
        for when, copies in waits:

            @pl.when(when)
            def _(copies=copies):
                for d in copies:
                    d.wait()

    return wait


def attend_kernel(kind, plan, n_piece, *refs):
    coord, mask_ref, hid_ref, cot_ref, wqkv_ref, wout_ref, edge_ref = refs[:7]
    pieces = refs[7 : 7 + n_piece]
    outs = refs[7 + n_piece : -5]
    w, wo, g4, sem, own_sem = refs[-5:]
    keep_ref, send_ref = outs[:2]
    core, zl, y = coord[0], coord[1], coord[2]
    cols = slice(kind * TOFF, kind * TOFF + HALF)
    wait = load_weights(plan, pieces, w, wo, sem, coord)
    rows = pl.ds(pl.multiple_of((zl * 4 + y) * ROWS, 16), ROWS)
    copies = []
    for t in range(3):
        if kind == 0:
            src, dst = wqkv_ref.at[:, t * D : t * D + HALF], w.at[t, rows, :]
        else:
            src, dst = wqkv_ref.at[:, t * D + HALF : (t + 1) * D], w.at[t, rows, 128:]
            copies.append(pltpu.make_async_copy(edge_ref.at[t], w.at[t, :, 0:128], own_sem.at[4 + t]))
        copies.append(pltpu.make_async_copy(src, dst, own_sem.at[t]))
    if kind == 0:
        copies.append(pltpu.make_async_copy(wout_ref, wo.at[rows, :], own_sem.at[3]))
    else:
        copies.append(pltpu.make_async_copy(wout_ref, wo, own_sem.at[3]))
    for c in copies:
        c.start()
    if kind == 1:
        normed, _ = normalize(hid_ref[:, :D])
        hid = normed.astype(BF)
        cot = hid_ref[:, D:]
        outs[3][...] = normed.T.astype(BF)
        outs[4][...] = cot
    else:
        hid, cot = hid_ref[...], cot_ref[...]
    for c in copies:
        c.wait()
    wait()
    if kind == 0:
        backs = [pltpu.make_async_copy(wo, outs[4], own_sem.at[3])]
        for t in range(3):
            backs.append(pltpu.make_async_copy(w.at[t, :, TOFF:HALF], outs[5].at[t], own_sem.at[t]))
        for c in backs:
            c.start()
    factor = 1.0 / math.sqrt(HEAD_SIZE)
    q = nn(hid, w[0]).astype(BF)
    k = nn(hid, w[1]).astype(BF)
    v = nn(hid, w[2]).astype(BF)
    u = nt(cot, wo[cols, :]).astype(BF)
    allowed = mask_ref[kind] > 0
    sums = [[None] * 5 for _ in range(4)]
    for h in range(8):
        s = kind * 64 + HEAD_SIZE * h
        t0, t1 = s // 128, (s + HEAD_SIZE - 1) // 128 + 1
        win = slice(t0 * 128, t1 * 128)
        lane = lax.broadcasted_iota(jnp.int32, (1, (t1 - t0) * 128), 1) + t0 * 128
        ours = jnp.logical_and(lane >= s, lane < s + HEAD_SIZE).astype(F32).astype(BF)
        qh, kh, vh, uh = (a[:, win] * ours for a in (q, k, v, u))
        sc = jnp.where(allowed, nt(kh, qh) * factor, NEG)
        e = jnp.exp(sc - jnp.max(sc, 0, keepdims=True))
        p = e * (1.0 / jnp.sum(e, 0, keepdims=True))
        pb = p.astype(BF)
        gp = nt(vh, uh)
        pg = p * gp
        gs = ((pg - p * jnp.sum(pg, 0, keepdims=True)) * factor).astype(BF)
        res = (tn(gs, kh), nn(gs, qh), nn(pb, uh), tn(pb, vh))
        for j, r in enumerate(res):
            for t in range(t0, t1):
                part = r[:, (t - t0) * 128 : (t - t0 + 1) * 128]
                sums[j][t] = part if sums[j][t] is None else sums[j][t] + part
        for t in range(5):
            if s < (t + 1) * 128 <= s + HEAD_SIZE or (h == 7 and t == 4):
                for j in range(4):
                    g4[j // 2, j % 2, :, t * 128 : (t + 1) * 128] = sums[j][t].astype(BF)
    gh = nt(g4[0, 0], w[0]) + nt(g4[0, 1], w[1]) + nt(g4[1, 0], w[2])
    if kind == 0:
        outs[2][...] = g4[1, 1]
        outs[3][...] = gh
    else:
        outs[2][:, :HALF] = g4[1, 1]
        outs[2][:, HALF:] = gh.astype(BF)
    keep_ref[...] = g4[core]
    send_ref[...] = g4[1 - core]
    if kind == 0:
        for c in backs:
            c.wait()


def attend_call(kind, coord, mask, hid, cot, w_qkv, w_out, edge, pieces, plan):
    s = jax.ShapeDtypeStruct
    both = s((2, TOK, HALF), BF)
    if kind == 0:
        outs, specs = (s((TOK, HALF), BF), s((TOK, D), F32), s((D, D), BF), s((3, D, 128), BF)), (VM, VM, HBM, HBM)
    else:
        outs, specs = (s((TOK, HALF + D), BF), s((D, TOK), BF), s((TOK, D), BF)), (VM,) * 3
    return pl.pallas_call(
        lambda *refs: attend_kernel(kind, plan, len(pieces), *refs),
        out_shape=(both, both) + outs,
        in_specs=[SM] + [VM] * 3 + [HBM] * (3 + len(pieces)),
        out_specs=(VM, VM) + specs,
        scratch_shapes=[
            pltpu.VMEM((3, D, HALF), BF),
            pltpu.VMEM((D, D), BF),
            pltpu.VMEM((2, 2, TOK, HALF), BF),
            pltpu.SemaphoreType.DMA((len(plan), 2)),
            pltpu.SemaphoreType.DMA((7,)),
        ],
        compiler_params=PARAMS,
        cost_estimate=pl.CostEstimate(flops=6 * 10**9, bytes_accessed=16 * 10**6, transcendentals=10**6),
        name=("attend_space", "attend_time")[kind],
    )(coord, mask, hid, cot, w_qkv, w_out, edge, *pieces)


SHIP0 = ((0, (1, 2)), (0, (0, 3)), (1, (3, 2)), (1, (0, 1)))
SHIP1 = ((1, (0, 1)), (1, (2, 3)), (0, (0, 1, 2, 3)))


def weight_kernel(index, coord, hft, hpt, hft2, hpt2, cf, cp, cf2, cp2, kf, kp, rf, rp, *refs):
    outs, (held, sem) = refs[:-2], refs[-2:]
    core, zl, y = coord[0], coord[1], coord[2]

    def by_hidden(x, out):
        tiles = [((0, 256), None), ((256, 512), None), ((512, 640), (0, 128)), (None, (128, 384)), (None, (384, 640))]
        at = 0
        for f, p in tiles:
            parts = []
            if f is not None:
                sl = slice(*f)
                parts += [nn(hft[...], kf[x, :, sl]), nn(hft2[...], rf[x, :, sl])]
            if p is not None:
                sl = slice(*p)
                parts += [nn(hpt[...], kp[x, :, sl]), nn(hpt2[...], rp[x, :, sl])]
            total = sum(parts[1:], parts[0])
            out[:, at : at + total.shape[1]] = total.astype(BF)
            at += total.shape[1]

    def by_attended(x, out):
        for c in range(0, D, 384):
            sl = slice(c, c + 384)
            f = tn(kf[x], cf[:, sl]) + tn(rf[x], cf2[:, sl])
            p = tn(kp[x], cp[:, sl]) + tn(rp[x], cp2[:, sl])
            out[0:512, sl] = f[:512].astype(BF)
            out[512:640, sl] = (f[512:] + p[:128]).astype(BF)
            out[640:1152, sl] = p[128:].astype(BF)

    if index == 0:
        by_hidden(0, held)
    else:

        @pl.when(core == 0)
        def _():
            by_hidden(1, held)

        @pl.when(core == 1)
        def _():
            by_attended(1, held)

    copies = []
    for r, ((a, order), out) in enumerate(zip((SHIP0, SHIP1)[index], outs)):
        for i, j in enumerate(order):
            rep = lax.rem(zl + a, 2) * 4 + jnp.bitwise_xor(y, j)
            rows = pl.ds(pl.multiple_of(rep * ROWS, 16), ROWS)
            c = pltpu.make_async_copy(held.at[rows, :], out.at[i], sem.at[r, i])
            c.start()
            copies.append(c)
    for c in copies:
        c.wait()


def weight_call(index, coord, *args):
    outs = tuple(jax.ShapeDtypeStruct((len(o), ROWS, D), BF) for _, o in (SHIP0, SHIP1)[index])
    cot = HBM if index == 0 else VM
    return pl.pallas_call(
        lambda *refs: weight_kernel(index, *refs),
        out_shape=outs,
        in_specs=[SM] + [VM] * 4 + [cot] * 4 + [VM] * 4,
        out_specs=(HBM,) * len(outs),
        scratch_shapes=[pltpu.VMEM((D, D), BF), pltpu.SemaphoreType.DMA((4, 4))],
        compiler_params=PARAMS,
        cost_estimate=pl.CostEstimate(flops=3 * 10**9, bytes_accessed=8 * 10**6, transcendentals=0),
        name="weight_grads",
    )(coord, *args)


def finish_kernel(lat_ref, cot_ref, att_ref, ghf_ref, back_ref, wo_ref, out_ref, gl_ref):
    lat = lat_ref[...]
    mixed = nn(att_ref[...], wo_ref[0:HALF, :]) + nn(back_ref[:, :HALF], wo_ref[TOFF:D, :])
    out_ref[...] = (lat.astype(F32) + mixed).astype(BF)
    normed, r = normalize(lat)
    gh = ghf_ref[...] + back_ref[:, HALF:].astype(F32)
    mean = jnp.mean(gh, -1, keepdims=True)
    dot = jnp.mean(gh * normed, -1, keepdims=True)
    gl_ref[...] = (cot_ref[...].astype(F32) + r * (gh - mean - normed * dot)).astype(BF)


def finish_call(*args):
    s = jax.ShapeDtypeStruct((TOK, D), BF)
    return pl.pallas_call(
        finish_kernel,
        out_shape=(s, s),
        in_specs=[VM] * 6,
        out_specs=(VM, VM),
        compiler_params=PARAMS,
        cost_estimate=pl.CostEstimate(flops=10**9, bytes_accessed=8 * 10**6, transcendentals=0),
        name="finish",
    )(*args)


def pairs(move):
    out = []
    for x in range(4):
        for z in range(8):
            for c in range(2):
                for y in range(4):
                    to = move(x, y, z, c)
                    spot = []
                    for xx, yy, zz, cc in ((x, y, z, c), (to[0] % 4, to[1] % 4, to[2] % 8, to[3])):
                        spot.append(((xx * 4 + zz // 2) * 2 + cc) * 8 + (zz % 2) * 4 + yy)
                    out.append(tuple(spot))
    return out


CORE = pairs(lambda x, y, z, c: (x, y, z, 1 - c))
XP = [pairs(lambda x, y, z, c, d=d: (x + d, y, z, c)) for d in range(4)]
YP = [pairs(lambda x, y, z, c, d=d: (x, y + d, z, c)) for d in range(4)]
ZP = [pairs(lambda x, y, z, c, d=d: (x, y, z + d, c)) for d in range(8)]
Y1 = pairs(lambda x, y, z, c: (x, y ^ 1, z, c))
Y3 = pairs(lambda x, y, z, c: (x, y ^ 3, z, c))
Z1 = pairs(lambda x, y, z, c: (x, y, z ^ 1, c))
Z1B = pairs(lambda x, y, z, c: (x, y, (z + 1 if z % 2 else z - 1), c))


def move(a, p):
    return lax.ppermute(a, AXES, p)


def add(*terms):
    total = terms[0].astype(F32)
    for t in terms[1:]:
        total = total + t.astype(F32)
    return total


def gather_weights(coord, w_qkv, w_out, early):
    e, g, z0, z1 = pack_call(coord, w_qkv, w_out)
    e_pieces, e_plan, g_pieces, g_plan = [], [], [], []

    def note(pieces, plan, array, parts):
        for other in (False, True):
            i = len(pieces)
            pieces.append(move(array, CORE) if other else array)
            for n, (name, dz, dy) in enumerate(parts):
                plan.append((lambda r, i=i, n=n: r[i].at[n], name, other, dz, dy))

    up, down = move(e, YP[1]), move(e, YP[3])
    z0, z1 = move(z0, ZP[1]), move(z1, ZP[7])
    z = jnp.stack([z0[:, :768], z1[:, :768]])
    gz = jnp.concatenate([z0[:, 768:], z1[:, 768:]], 1)
    zup, zdown = move(z, YP[1]), move(z, YP[3])
    up, down, *early = lax.optimization_barrier((up, down, *early))
    lat_cot, *early = early
    pos = lax.all_to_all(lat_cot, "tm", split_axis=0, concat_axis=0, tiled=True).reshape(TOK, 2 * D)
    relays = [move(up[0], YP[1]), move(down[1], YP[3]), move(zup[0], YP[1]), move(zdown[1], YP[3])]
    *relays, g, gz = lax.optimization_barrier((*relays, g, gz))
    gg = jnp.stack([g, gz])
    g_all = (gz[None], move(gg, YP[1]), move(gg, YP[3]), move(gg, YP[2]))
    for array, dz, dy in ((z, 1, 0), (up, 0, 3), (down, 0, 1), (zup, 1, 3), (zdown, 1, 1)):
        note(e_pieces, e_plan, array, (("e0", dz, dy), ("e1", dz, dy)))
    for n, array in enumerate(relays):
        note(e_pieces, e_plan, array[None], ((("e0", "e1")[n % 2], n // 2, 2),))

    def second(after):
        after, *arrays = lax.optimization_barrier((after, *g_all))
        note(g_pieces, g_plan, arrays[0], (("g", 1, 0),))
        for array, dy in zip(arrays[1:], (3, 1, 2)):
            note(g_pieces, g_plan, array, (("g", 0, dy), ("g", 1, dy)))
        return after, g_pieces, g_plan

    return (e_pieces, e_plan), second, pos, early


def all_sum(own):
    x = lax.axis_index("tm") // 8
    parts = own.reshape(4, 72, D)

    def part(i):
        return lax.dynamic_index_in_dim(parts, i % 4, 0, keepdims=False)

    got = [move(part(x + d), XP[d]) for d in (1, 2, 3)]
    mine = add(part(x), *got).astype(BF)
    two, four, six = (move(mine, ZP[d]) for d in (2, 4, 6))
    row = (add(mine, four) + add(two, six)).astype(BF)
    ring = jnp.stack([row] + [move(row, XP[d]) for d in (1, 2, 3)])
    return jnp.take(ring, (x - jnp.arange(4)) % 4, axis=0).reshape(2, ROWS, D)


def reduce_out0(s0a, k0a, s0b, k0b):
    ga, gb = move(s0a, Y1), move(s0b, Y3)
    ka, kb = add(k0a, ga).astype(BF), add(k0b, gb).astype(BF)
    ga, gb = move(ka[1], Y3), move(kb[1], Y1)
    ours, theirs = add(ka[0], ga), add(kb[0], gb).astype(BF)
    ga, gb = move(theirs[:72], Z1), move(theirs[72:], Z1B)
    return jnp.concatenate([add(ours[:72], ga), add(ours[72:], gb)]).astype(BF)


def reduce_out1(sa, sb, keep):
    ga, gb = move(sa, Z1), move(sb, Z1B)
    b = [add(keep[0], ga[0]), add(keep[1], ga[1]), add(keep[2], gb[0]), add(keep[3], gb[1])]
    b = [t.astype(BF) for t in b]
    top, low = [t[:72] for t in b], [t[72:] for t in b]
    gt = move(jnp.stack([top[1], top[2]]), Y1)
    gl = move(jnp.stack([low[3], low[2]]), Y3)
    t0, t3 = add(top[0], gt[0]).astype(BF), add(top[3], gt[1]).astype(BF)
    l0, l1 = add(low[0], gl[0]).astype(BF), add(low[1], gl[1]).astype(BF)
    gt, gl = move(t3, Y3), move(l1, Y1)
    return jnp.concatenate([add(t0, gt), add(l0, gl)]).astype(BF)


def local(latents, cotangent, w_qkv, w_out, tile_pattern):
    tm, rep = lax.axis_index("tm"), lax.axis_index("replica")
    core, zl, y = tm % 2, rep // 4, rep % 4
    coord = jnp.stack([core, zl, y]).astype(jnp.int32)
    lat, cot = latents.reshape(TOK, D), cotangent.reshape(TOK, D)
    lat_cot = jnp.concatenate([lat, cot], 1).reshape(32, 8, 2 * D)
    early = (lat_cot, *norm_call(tile_pattern, lat), move(cot, CORE))
    e_part, second, pos, early = gather_weights(coord, w_qkv, w_out, early)
    hf, hft, mask, cf2 = early

    kf, sf, att, ghf, wo, edge = attend_call(0, coord, mask, hf, cot, w_qkv, w_out, w_out, *e_part)
    edge, *g_part = second(edge)
    rf, hft2 = move(sf, CORE), move(hft, CORE)
    kp, sp, back, hpt, cp = attend_call(1, coord, mask, pos, cot, w_qkv, wo, edge, *g_part)
    sp, rf, hft2 = lax.optimization_barrier((sp, rf, hft2))
    rp, hpt2, cp2 = move(sp, CORE), move(hpt, CORE), move(cp, CORE)
    terms = (coord, hft, hpt, hft2, hpt2, cot, cp, cf2, cp2, kf, kp, rf, rp)
    w0, w1 = weight_call(0, *terms), weight_call(1, *terms)
    *w1, back = lax.optimization_barrier((*w1, back))
    back = lax.all_to_all(
        back.reshape(32, 8, HALF + D), "tm", split_axis=0, concat_axis=0, tiled=True
    ).reshape(TOK, HALF + D)
    own = jnp.concatenate([reduce_out0(*w0), reduce_out1(*w1)])
    own, back = lax.optimization_barrier((own, back))
    result, grad_input = finish_call(lat, cot, att, ghf, back, wo)
    total = all_sum(own)
    other = move(total, CORE)
    factor = 1.0 / math.sqrt(65536)
    first = core == 0
    q, k = (jnp.where(first, total[i], other[i]) for i in range(2))
    v, o = (jnp.where(first, other[i], total[i]) for i in range(2))
    dw_qkv = jnp.concatenate([q, k, v], 1).astype(F32) * factor
    dw_out = o.astype(F32) * factor
    return result.reshape(1, 1, TOK, D), grad_input.reshape(1, 1, TOK, D), dw_qkv, dw_out


def solution(mesh):
    tokens, rows = P("replica", "tm", None, None), P("replica", None)
    return jax.shard_map(
        local,
        mesh=mesh,
        in_specs=(tokens, tokens, rows, rows, P()),
        out_specs=(tokens, tokens, rows, rows),
        check_vma=False,
    )
```
